256 devices in a mesh: dp: 8 (over y, core), expert: 32 (over x, z).
Axes of the slice: x: 4, y: 4, z: 8, core: 2. Of those that a mesh axis runs over, the one named last changes fastest.
Arguments:
- tokens: bfloat16 [32768, 4096], P(('dp', 'expert')), may hold values from -6 to 6
- cotangent: bfloat16 [32768, 4096], P(('dp', 'expert')), may hold values from -1.5 to 1.5
- picks: int32 [8, 32, 64], P('dp'), may hold values from 0 to 4095, as said below
- gate_values: bfloat16 [8, 32, 64], P('dp', 'expert'), may hold values from 0.099609375 to 1
- w_gate: bfloat16 [32, 4096, 1536], P('expert', None, 'dp'), may hold values from -0.09375 to 0.09375
- w_up: bfloat16 [32, 4096, 1536], P('expert', None, 'dp'), may hold values from -0.09375 to 0.09375
- w_down: bfloat16 [32, 1536, 4096], P('expert', 'dp'), may hold values from -0.15625 to 0.15625
Outputs:
- d_tokens: bfloat16 [32768, 4096], P(('dp', 'expert'))
- d_gate_values: float32 [8, 32, 64], P('dp', 'expert')
- d_w_gate: bfloat16 [32, 4096, 1536], P('expert', None, 'dp')
- d_w_up: bfloat16 [32, 4096, 1536], P('expert', None, 'dp')
- d_w_down: bfloat16 [32, 1536, 4096], P('expert', 'dp')
The draws below stay inside these ranges and needn't reach their ends.
Inputs may be any that keep to these rules, and one draw needn't show every extreme that they name: For each group and expert the 64 positions are distinct. Among the 128 tokens of any one device of a group, one expert picks at most 4, and in every group each expert picks exactly 4 from some device.
All inputs are finite; a program needn't handle non-finite values.
Results may differ from the reference program's by a relative error of at most 0.0057.
Values may be sent and summed in bfloat16 or wider, within the bound.
A program may use at most 128 MiB of HBM per device.

```python
import jax
import jax.numpy as jnp
from jax import lax

D = 4096
FF = 1536
TOK_DEV = 128
CAP = 64
GROUPS = 8
EXPERTS = 32
TOK_GROUP = 4096
TOKENS = 32768


def draw_picks(key, part):
    first, second, third, fourth = jax.random.split(key, 4)
    base = CAP // EXPERTS
    pairs = EXPERTS // 2
    order = jax.vmap(lambda k: jax.random.permutation(k, EXPERTS))(jax.random.split(first, GROUPS * EXPERTS))
    order = order.reshape(GROUPS, EXPERTS, EXPERTS)
    delta = jax.random.randint(second, (GROUPS, EXPERTS, pairs), -base, base + 1)
    delta = delta.at[:, :, 0].set(base)
    bump = jnp.concatenate([delta, -delta], axis=2)
    onehot = (order[:, :, :, None] == jnp.arange(EXPERTS)[None, None, None, :]).astype(jnp.int32)
    counts = base + jnp.sum(bump[:, :, :, None] * onehot, axis=2)
    ends = jnp.cumsum(counts, axis=-1)
    starts = ends - counts
    slot = jnp.arange(CAP)
    shard_of = jnp.sum((ends[:, :, None, :] <= slot[:, None]).astype(jnp.int32), axis=-1)
    start_of = jnp.take_along_axis(starts, shard_of, axis=-1)
    rank = slot[None, None, :] - start_of
    inner = jax.vmap(lambda k: jax.random.permutation(k, TOK_DEV))(jax.random.split(third, GROUPS * EXPERTS * EXPERTS))
    inner = inner.reshape(GROUPS, EXPERTS, EXPERTS * TOK_DEV)
    position = jnp.take_along_axis(inner, shard_of * TOK_DEV + rank, axis=-1)
    token = shard_of * TOK_DEV + position
    shuffle = jax.vmap(lambda k: jax.random.permutation(k, CAP))(jax.random.split(fourth, GROUPS * EXPERTS))
    shuffle = shuffle.reshape(GROUPS, EXPERTS, CAP)
    return jnp.take_along_axis(token, shuffle, axis=-1).astype(jnp.int32)


def level_of(key, shape, cuts, least, largest):
    def one(axis_at, parts):
        draws = jax.random.uniform(jax.random.fold_in(jax.random.fold_in(key, 6), axis_at), (parts,), jnp.float32, least / len(cuts), largest / len(cuts))
        return jnp.repeat(jnp.exp(draws), shape[axis_at] // parts).reshape((-1,) + (1,) * (len(shape) - axis_at - 1))

    factor_of = one(*cuts[0])
    for cut in cuts[1:]:
        factor_of = factor_of * one(*cut)
    return factor_of


def normal_values(own_key, dims, width, reach, cuts=(), held_as=jnp.bfloat16):
    values = width * jax.random.normal(own_key, dims, jnp.float32)
    if cuts:
        values = values * level_of(own_key, dims, cuts, -0.22, 0.18)
    return jnp.clip(values, -reach, reach).astype(held_as)


def setup_inputs(seed: int = 0) -> dict:
    key_list = jax.random.split(jax.random.key(seed), 8)
    tokens = normal_values(key_list[0], (TOKENS, D), 1.0, 6.0, ((0, 256),))
    cotangent = normal_values(key_list[1], (TOKENS, D), 0.25, 1.5, ((0, 256),))
    picks = draw_picks(jax.random.fold_in(key_list[7], 71), 0)
    gate_values = jnp.clip(0.099609375 + 0.9003906 * jax.random.uniform(key_list[3], (GROUPS, EXPERTS, CAP), jnp.float32) ** level_of(key_list[3], (GROUPS, EXPERTS, CAP), ((0, 8), (1, 32)), -0.2, 0.2), 0.099609375, 1.0).astype(jnp.bfloat16)
    w_gate = normal_values(key_list[4], (EXPERTS, D, FF), D ** -0.5, 0.09375, ((0, 32), (2, 8)))
    w_up = normal_values(key_list[5], (EXPERTS, D, FF), D ** -0.5, 0.09375, ((0, 32), (2, 8)))
    w_down = normal_values(key_list[6], (EXPERTS, FF, D), FF ** -0.5, 0.15625, ((0, 32), (1, 8)))
    return {"tokens": tokens, "cotangent": cotangent, "picks": picks, "gate_values": gate_values, "w_gate": w_gate, "w_up": w_up, "w_down": w_down}


def expert_grads(rows, dyr, gv, wg, wu, wd):
    gate = jnp.dot(rows, wg, preferred_element_type=jnp.float32)
    up = jnp.dot(rows, wu, preferred_element_type=jnp.float32)
    act = jax.nn.silu(gate)
    hidden = (act * up).astype(jnp.bfloat16)
    out = jnp.dot(hidden, wd, preferred_element_type=jnp.float32)
    score = jnp.sum(out * dyr.astype(jnp.float32), axis=-1)
    back = jnp.dot(dyr, wd.T, preferred_element_type=jnp.float32)
    d_hidden = gv[:, None] * back
    sig = jax.nn.sigmoid(gate)
    d_gate = (d_hidden * up * sig * (1.0 + gate * (1.0 - sig))).astype(jnp.bfloat16)
    d_up = (d_hidden * act).astype(jnp.bfloat16)
    d_out = (gv[:, None] * dyr.astype(jnp.float32)).astype(jnp.bfloat16)
    dwd = jnp.dot(hidden.T, d_out, preferred_element_type=jnp.float32).astype(jnp.bfloat16)
    dwg = jnp.dot(rows.T, d_gate, preferred_element_type=jnp.float32).astype(jnp.bfloat16)
    dwu = jnp.dot(rows.T, d_up, preferred_element_type=jnp.float32).astype(jnp.bfloat16)
    d_rows = jnp.dot(d_gate, wg.T, preferred_element_type=jnp.float32)
    d_rows = d_rows + jnp.dot(d_up, wu.T, preferred_element_type=jnp.float32)
    return dwg, dwu, dwd, score, d_rows.astype(jnp.bfloat16)


def reference(tokens, cotangent, picks, gate_values, w_gate, w_up, w_down):
    grouped = tokens.reshape(GROUPS, TOK_GROUP, D)
    grouped_dy = cotangent.reshape(GROUPS, TOK_GROUP, D)
    lists = jnp.transpose(picks, (1, 0, 2))
    gates = jnp.transpose(gate_values, (1, 0, 2))

    def one_expert(inputs):
        index, gv, wg, wu, wd = inputs
        rows = jax.vmap(lambda table, where: table[where])(grouped, index).reshape(GROUPS * CAP, D)
        dyr = jax.vmap(lambda table, where: table[where])(grouped_dy, index).reshape(GROUPS * CAP, D)
        return expert_grads(rows, dyr, gv.reshape(GROUPS * CAP).astype(jnp.float32), wg, wu, wd)

    dwg, dwu, dwd, score, d_rows = lax.map(one_expert, (lists, gates, w_gate, w_up, w_down))
    d_rows = d_rows.reshape(EXPERTS, GROUPS, CAP, D)
    d_gate_values = jnp.transpose(score.reshape(EXPERTS, GROUPS, CAP), (1, 0, 2))
    pieces = []
    for group in range(GROUPS):
        total = jnp.zeros((TOK_GROUP, D), jnp.float32)
        total = total.at[picks[group].reshape(-1)].add(d_rows[:, group].reshape(EXPERTS * CAP, D).astype(jnp.float32))
        pieces.append(total.astype(jnp.bfloat16))
    d_tokens = jnp.concatenate(pieces, axis=0)
    return d_tokens, d_gate_values, dwg, dwu, dwd
```

```python
import jax
import jax.numpy as jnp
from jax import lax
from jax.sharding import PartitionSpec as P


def on_device(tokens, cotangent, picks, gate_values, w_gate, w_up, w_down):
    tok_rows, width = tokens.shape
    shards = lax.axis_size("expert")
    own_index = lax.axis_index("expert")
    lists = picks[0]
    capacity = lists.shape[1]
    most = 2 * (capacity // shards)
    source = lists // tok_rows
    local = lists % tok_rows
    same = source[:, :, None] == source[:, None, :]
    before = jnp.arange(capacity)[None, :] < jnp.arange(capacity)[:, None]
    rank = jnp.sum((same & before[None, :, :]).astype(jnp.int32), axis=-1)
    mine = source == own_index
    slot_hot = (mine[:, None, :] & (rank[:, None, :] == jnp.arange(most)[None, :, None])).astype(
        jnp.int32
    )
    slot_index = jnp.sum(slot_hot * local[:, None, :], axis=-1)
    slot_valid = jnp.sum(slot_hot, axis=-1) > 0
    keep = slot_valid[:, :, None]
    send_rows = jnp.where(keep, tokens[slot_index], jnp.zeros((), jnp.bfloat16))
    send_dy = jnp.where(keep, cotangent[slot_index], jnp.zeros((), jnp.bfloat16))
    recv_rows, recv_dy = (
        lax.all_to_all(send_rows, "expert", split_axis=0, concat_axis=0, tiled=True),
        lax.all_to_all(send_dy, "expert", split_axis=0, concat_axis=0, tiled=True),
    )
    my_source = lax.dynamic_index_in_dim(source, own_index, 0, keepdims=False)
    my_rank = lax.dynamic_index_in_dim(rank, own_index, 0, keepdims=False)
    flat = my_source * most + my_rank
    rows = recv_rows.reshape(shards * most, width)[flat]
    dyr = recv_dy.reshape(shards * most, width)[flat]
    all_rows, all_dy, all_gv = (
        lax.all_gather(rows, "dp", axis=0, tiled=True),
        lax.all_gather(dyr, "dp", axis=0, tiled=True),
        lax.all_gather(gate_values[0, 0], "dp", axis=0, tiled=True),
    )
    w_g = w_gate[0]
    w_u = w_up[0]
    w_d = w_down[0]
    gate = jnp.dot(all_rows, w_g, preferred_element_type=jnp.float32)
    up = jnp.dot(all_rows, w_u, preferred_element_type=jnp.float32)
    act = jax.nn.silu(gate)
    hidden = (act * up).astype(jnp.bfloat16)
    back = lax.dot_general(
        all_dy, w_d, (((1,), (1,)), ((), ())), preferred_element_type=jnp.float32
    )
    score_part = jnp.sum(hidden.astype(jnp.float32) * back, axis=-1)
    score = lax.psum_scatter(score_part, "dp", scatter_dimension=0, tiled=True)
    gv = all_gv.astype(jnp.float32)
    d_hidden = gv[:, None] * back
    sig = jax.nn.sigmoid(gate)
    d_gate = (d_hidden * up * sig * (1.0 + gate * (1.0 - sig))).astype(jnp.bfloat16)
    d_up = (d_hidden * act).astype(jnp.bfloat16)
    d_out = (gv[:, None] * all_dy.astype(jnp.float32)).astype(jnp.bfloat16)
    contract_rows = (((0,), (0,)), ((), ()))
    dwd = lax.dot_general(hidden, d_out, contract_rows, preferred_element_type=jnp.float32).astype(
        jnp.bfloat16
    )
    dwg = lax.dot_general(
        all_rows, d_gate, contract_rows, preferred_element_type=jnp.float32
    ).astype(jnp.bfloat16)
    dwu = lax.dot_general(all_rows, d_up, contract_rows, preferred_element_type=jnp.float32).astype(
        jnp.bfloat16
    )
    contract_hidden = (((1,), (1,)), ((), ()))
    total = lax.dot_general(d_gate, w_g, contract_hidden, preferred_element_type=jnp.float32)
    d_pick = lax.psum_scatter(
        (
            total + lax.dot_general(d_up, w_u, contract_hidden, preferred_element_type=jnp.float32)
        ).astype(jnp.bfloat16),
        "dp",
        scatter_dimension=0,
        tiled=True,
    ).astype(jnp.bfloat16)
    back_slots = jnp.zeros((shards * most, width), jnp.bfloat16).at[flat].set(d_pick)
    returned = lax.all_to_all(
        back_slots.reshape(shards, most, width), "expert", split_axis=0, concat_axis=0, tiled=True
    )
    token_hot = slot_valid[None, :, :] & (
        slot_index[None, :, :] == jnp.arange(tok_rows)[:, None, None]
    )
    token_hot = token_hot.reshape(tok_rows, shards * most).astype(jnp.bfloat16)
    d_tokens = jnp.dot(
        token_hot, returned.reshape(shards * most, width), preferred_element_type=jnp.float32
    )
    return (
        d_tokens.astype(jnp.bfloat16),
        score.reshape(1, 1, capacity),
        dwg[None],
        dwu[None],
        dwd[None],
    )


def solution(mesh):
    in_specs = (
        P(("dp", "expert"), None),
        P(("dp", "expert"), None),
        P("dp", None, None),
        P("dp", "expert", None),
        P("expert", None, "dp"),
        P("expert", None, "dp"),
        P("expert", "dp", None),
    )
    out_specs = (
        P(("dp", "expert"), None),
        P("dp", "expert", None),
        P("expert", None, "dp"),
        P("expert", None, "dp"),
        P("expert", "dp", None),
    )
    return jax.shard_map(
        on_device, mesh=mesh, in_specs=in_specs, out_specs=out_specs, check_vma=False
    )
```

```python
import functools

import jax
import jax.numpy as jnp
from jax import lax
from jax.experimental import pallas as pl
from jax.experimental.pallas import tpu as pltpu
from jax.sharding import PartitionSpec as P

MESH = pl.DeviceIdType.MESH
BF = jnp.bfloat16
F32 = jnp.float32
NT = (((1,), (1,)), ((), ()))
SLOTS = 4
SUB = 4
ROWS = SLOTS * SUB
CH = 2
RC = 2


def dot(a, b):
    return jnp.dot(a, b, preferred_element_type=F32)


def dot_nt(a, b):
    return lax.dot_general(a, b, NT, preferred_element_type=F32)


def al(i, m):
    return pl.multiple_of(i, m)


def kernel(
    experts, tok, cot, picks, gates, wg_h, wu_h, wd_h,
    dtok, score, dwg_h, dwu_h, dwd_h,
    sendb, recvb, alls, gvb, gv_all, wg, wu, wd, wsib, gate, up, back, dgu, dgs, tr,
    a_s, a_r, b_s, b_r, dg_own, dg_x, ret_s, ret_r, sc_p, sc_r, dwg, dwu, dwd,
    d_send, d_recv, g_send, g_recv, small_s, small_r, sib_s, sib_r, rs_s, rs_r, r_send, r_recv, loc,
):
    tok_rows, width = tok.shape
    cap = gvb.shape[0]
    dp = lax.axis_index("dp")
    ex = lax.axis_index("expert")
    y = dp // 2
    k = lax.rem(dp, 2)
    y_up, y_dn, y_op = lax.rem(y + 1, 4), lax.rem(y + 3, 4), lax.rem(y + 2, 4)
    up_d, dn_d, op_d, sib = y_up * 2 + k, y_dn * 2 + k, y_op * 2 + k, y * 2 + 1 - k
    half = width // 2
    cw = width // CH
    sw = cw // SUB
    nrow = experts * ROWS

    loads = [
        pltpu.make_async_copy(h.at[0], v, loc.at[i])
        for i, (h, v) in enumerate(((wg_h, wg), (wu_h, wu), (wd_h, wd)))
    ]
    for c in loads:
        c.start()

    pending = []
    barrier = pltpu.get_barrier_semaphore()

    def hail(d, carry):
        pl.semaphore_signal(
            barrier, inc=1, device_id=(dp, lax.rem(ex + d, experts)), device_id_type=MESH
        )
        return carry

    def hail_dp(d, carry):
        pl.semaphore_signal(
            barrier, inc=1, device_id=(lax.rem(dp + d, 8), ex), device_id_type=MESH
        )
        return carry

    lax.fori_loop(1, experts, hail, 0)
    lax.fori_loop(1, 8, hail_dp, 0)

    def copy(src, dst, s, r, to):
        return pltpu.make_async_remote_copy(
            src_ref=src, dst_ref=dst, send_sem=s, recv_sem=r, device_id=(to, ex), device_id_type=MESH
        )

    def push(src, dst, s, r, to):
        d = copy(src, dst, s, r, to)
        d.start()
        pending.append(d.wait_send)
        return d

    def spread(src, dst, s, r):
        def send(d, carry):
            to = lax.rem(ex + d, experts)
            pltpu.make_async_remote_copy(
                src_ref=src.at[pl.ds(al(to * ROWS, ROWS), ROWS)],
                dst_ref=dst.at[pl.ds(al(ex * ROWS, ROWS), ROWS)],
                send_sem=s, recv_sem=r, device_id=(dp, to), device_id_type=MESH,
            ).start()
            return carry

        lax.fori_loop(1, experts, send, 0)
        pending.append(lambda: await_bytes(src, s))

    def await_bytes(ref, sem):
        part = ref.at[pl.ds(0, nrow - ROWS)]
        pltpu.make_async_copy(part, part, sem).wait()

    shift = tok_rows.bit_length() - 1
    lists = picks[0]
    mine_f = jnp.where((lists >> shift) == ex, 1.0, 0.0)
    ahead = lax.broadcasted_iota(jnp.int32, (cap, cap), 0) < lax.broadcasted_iota(jnp.int32, (cap, cap), 1)
    place = dot(mine_f.astype(BF), jnp.where(ahead, 1.0, 0.0).astype(BF))
    token = ((lists & (tok_rows - 1)) + 1).astype(F32) * mine_f
    lane = lax.broadcasted_iota(jnp.int32, (experts, 128), 1)
    slots = jnp.zeros((experts, 128), F32)
    for s in range(SLOTS):
        at = jnp.sum(jnp.where(place == s, token, 0.0), axis=-1, keepdims=True)
        slots = jnp.where(lane == s, at, slots)
    grow = lax.broadcasted_iota(jnp.int32, (nrow, experts), 0) // ROWS
    spot = jnp.where(grow == lax.broadcasted_iota(jnp.int32, (nrow, experts), 1), 1.0, 0.0)
    spread_slots = dot(spot.astype(BF), slots.astype(BF))
    pick_lane = lax.rem(lax.broadcasted_iota(jnp.int32, (nrow, 128), 0), SLOTS)
    at_lane = lax.broadcasted_iota(jnp.int32, (nrow, 128), 1)
    sidx_c = jnp.sum(jnp.where(at_lane == pick_lane, spread_slots, 0.0), axis=-1, keepdims=True) - 1.0

    row_sub = lax.rem(lax.broadcasted_iota(jnp.int32, (nrow, tok_rows), 0) // SLOTS, SUB)
    col_tok = lax.broadcasted_iota(jnp.int32, (nrow, tok_rows), 1)
    match = sidx_c == col_tok.astype(F32)
    hots = [jnp.where(match & (row_sub == b), 1.0, 0.0).astype(BF) for b in range(SUB)]
    own = pl.ds(al(ex * ROWS, ROWS), ROWS)
    for q in range(2 * CH):
        src = tok if q < CH else cot
        base = (q % CH) * cw
        acc = dot(hots[0], src[:, base : base + sw])
        for b in range(1, SUB):
            acc += dot(hots[b], src[:, base + b * sw : base + (b + 1) * sw])
        sendb[q] = acc.astype(BF)
        recvb[q, own, :] = sendb[q, own, :]
        if q == 0:
            pl.semaphore_wait(barrier, experts - 1 + 7)
        spread(sendb.at[q], recvb.at[q], d_send.at[q], d_recv.at[q])

    own_row = picks[0, pl.ds(ex, 1), :]
    src_row = jnp.broadcast_to((own_row >> shift).astype(F32), (128, cap))
    src_col = src_row.T
    behind = lax.broadcasted_iota(jnp.int32, (cap, cap), 0) > lax.broadcasted_iota(jnp.int32, (cap, cap), 1)
    twins = jnp.where((src_col[:, :cap] == src_row[:cap]) & behind, 1.0, 0.0)
    rfl_c = src_col[:, 0:1] * ROWS + jnp.sum(twins, axis=-1, keepdims=True)
    rfl_r = jnp.broadcast_to(rfl_c, (cap, 128)).T[0:1]
    sidx_r = jnp.broadcast_to(sidx_c, (nrow, 128)).T[0:1]
    gvb[...] = jnp.broadcast_to(gates[0].astype(F32), (128, cap)).T

    mine = pl.ds(al(dp * cap, cap), cap)
    gv_all[mine, :] = gvb[...]

    def send_gv(d, carry):
        copy(gvb, gv_all.at[mine], small_s.at[0], small_r.at[0], lax.rem(dp + d, 8)).start()
        return carry

    lax.fori_loop(1, 8, send_gv, 0)
    gv_part = gv_all.at[pl.ds(0, 7 * cap)]
    pending.append(pltpu.make_async_copy(gv_part, gv_part, small_s.at[0]).wait)
    other = pl.ds(al((1 - k) * half, half), half)
    ws0 = push(wg_h.at[0, :, other], wsib.at[0], sib_s.at[0], sib_r.at[0], sib)
    ws1 = push(wu_h.at[0, :, other], wsib.at[1], sib_s.at[1], sib_r.at[1], sib)
    for c in loads:
        c.wait()

    lane_row = lax.broadcasted_iota(jnp.int32, (cap, nrow), 1).astype(F32)
    for q in range(2 * CH):
        a, c = q // CH, q % CH
        cols = pl.ds(c * cw, cw)

        def blk(i, lo=0, n=cap):
            return alls.at[a, pl.ds(al(i * cap + lo, 16), n), cols]

        def pass_on(j, i, to, lo=0, n=cap):
            return push(blk(i, lo, n), blk(i, lo, n), g_send.at[q, j], g_recv.at[q, j], to)

        await_bytes(recvb.at[q], d_recv.at[q])
        for b in range(SUB):
            rhot = jnp.where(rfl_c + b * SLOTS == lane_row, 1.0, 0.0).astype(BF)
            alls[a, mine, c * cw + b * sw : c * cw + (b + 1) * sw] = dot(rhot, recvb[q]).astype(BF)
        hc = cap // 2
        c_up = pass_on(0, dp, up_d)
        c_dn = pass_on(1, dp, dn_d)
        s0 = pass_on(2, dp, sib)
        c_up.wait_recv()
        f_up = pass_on(3, dn_d, up_d, 0, hc)
        s1 = pass_on(4, dn_d, sib)
        c_dn.wait_recv()
        f_dn = pass_on(5, up_d, dn_d, hc, hc)
        s2 = pass_on(6, up_d, sib)
        f_up.wait_recv()
        s3 = pass_on(7, op_d, sib, 0, hc)
        f_dn.wait_recv()
        s4 = pass_on(8, op_d, sib, hc, hc)
        for s in (s0, s1, s2, s3, s4):
            s.wait_recv()

        kt = 512

        if a == 0:
            if c == 0:
                gate[...] = jnp.zeros_like(gate)
                up[...] = jnp.zeros_like(up)

            def fwd(i, carry):
                kk = pl.ds(al(c * cw + i * kt, kt), kt)
                r = alls[0, :, kk]
                gate[...] += dot_nt(r, wg[:, kk])
                up[...] += dot_nt(r, wu[:, kk])
                return carry

            lax.fori_loop(0, cw // kt, fwd, 0)
        else:
            if c == 0:
                back[...] = jnp.zeros_like(back)

            def bwd(i, carry):
                kk = pl.ds(al(c * cw + i * kt, kt), kt)
                back[...] += dot_nt(alls[1, :, kk], wd[:, kk])
                return carry

            lax.fori_loop(0, cw // kt, bwd, 0)

    pltpu.make_async_copy(gv_part, gv_part, small_r.at[0]).wait()

    def pointwise(i, carry):
        r = pl.ds(al(i * 128, 128), 128)
        g, u, bk = gate[r, :], up[r, :], back[r, :]
        gv = gv_all[r, 0:1]
        s = jax.nn.sigmoid(g)
        act = g * s
        hidden = (act * u).astype(BF).astype(F32)
        sc_p[r, :] = jnp.broadcast_to(jnp.sum(hidden * bk, axis=-1, keepdims=True), (128, 128))
        dh = gv * bk
        dgate = (dh * u * s * (1.0 + g * (1.0 - s))).astype(BF)
        dup = (dh * act).astype(BF)
        dgu[0, r, :] = dgate
        dgu[1, r, :] = dup
        tr[0, :, r] = hidden.T.astype(BF)
        tr[1, :, r] = dgate.astype(F32).T.astype(BF)
        tr[2, :, r] = dup.astype(F32).T.astype(BF)
        return carry

    lax.fori_loop(0, 4, pointwise, 0)
    dx = push(dgu, dgs, sib_s.at[2], sib_r.at[2], sib)

    def send_score(d, carry):
        to = lax.rem(dp + d, 8)
        copy(
            sc_p.at[pl.ds(al(to * cap, cap), cap)], sc_r.at[lax.rem(8 - d, 8)],
            small_s.at[1], small_r.at[1], to,
        ).start()
        return carry

    lax.fori_loop(1, 8, send_score, 0)
    sc_part = sc_r.at[pl.ds(1, 7)]
    pending.append(pltpu.make_async_copy(sc_part, sc_part, small_s.at[1]).wait)
    ws0.wait_recv()
    ws1.wait_recv()
    dx.wait_recv()

    two = 2 * cap
    fw = half // RC
    hw = fw // 2

    def part(yy, c):
        r = pl.ds(al(yy * two, two), two)
        w_at = pl.ds(al(k * half + c * fw, fw), fw)
        o_at = pl.ds(c * fw, fw)
        t = dot(dgu[0, r, :], wg[:, w_at])
        t += dot(dgu[1, r, :], wu[:, w_at])
        t += dot(dgs[0, r, :], wsib[0, :, o_at])
        t += dot(dgs[1, r, :], wsib[1, :, o_at])
        return t

    a_cp, b_cp, x_cp = [], [], []
    for c in range(RC):
        t = part(y_op, c)
        a_s[c, 0] = t[:, :hw].astype(BF)
        a_s[c, 1] = t[:, hw:].astype(BF)
        for j, to in ((0, up_d), (1, dn_d)):
            a_cp.append(push(a_s.at[c, j], a_r.at[c, j], rs_s.at[c, j], rs_r.at[c, j], to))
    for c in range(RC):
        for j, (yy, to) in enumerate(((y_up, up_d), (y_dn, dn_d))):
            t = part(yy, c)
            a_cp[2 * c + j].wait_recv()
            at = slice(0, hw) if j == 0 else slice(hw, fw)
            rest = slice(hw, fw) if j == 0 else slice(0, hw)
            b_s[c, j, :, at] = (t[:, at] + a_r[c, j].astype(F32)).astype(BF)
            b_s[c, j, :, rest] = t[:, rest].astype(BF)
            b_cp.append(
                push(b_s.at[c, j], b_r.at[c, j], rs_s.at[c, 2 + j], rs_r.at[c, 2 + j], to)
            )
    for c in range(RC):
        t = part(y, c)
        b_cp[2 * c].wait_recv()
        b_cp[2 * c + 1].wait_recv()
        t += b_r[c, 0].astype(F32) + b_r[c, 1].astype(F32)
        dg_own[c] = t.astype(BF)
        x_cp.append(
            push(
                dg_own.at[c, pl.ds(al((1 - k) * cap, cap), cap)], dg_x.at[c],
                rs_s.at[c, 4], rs_r.at[c, 4], sib,
            )
        )

    row_i = lax.broadcasted_iota(jnp.int32, (nrow, cap), 0).astype(F32)
    for c in range(RC):
        x_cp[c].wait_recv()
        mine_half = dg_own[c, pl.ds(al(k * cap, cap), cap), :]
        theirs = dg_x[c]
        first = k == 0
        h0 = jnp.where(first, mine_half, theirs)
        h1 = jnp.where(first, theirs, mine_half)
        acc = jnp.zeros((nrow, hw), F32)
        for b in range(SUB):
            hot = jnp.where(rfl_r + b * SLOTS == row_i, 1.0, 0.0).astype(BF)
            src = h0 if b < 2 else h1
            acc += dot(hot, src[:, (b % 2) * hw : (b % 2 + 1) * hw])
        ret_s[c] = acc.astype(BF)
        ret_r[c, own, :] = ret_s[c, own, :]
        spread(ret_s.at[c], ret_r.at[c], r_send.at[c], r_recv.at[c])

    nt = 512

    def grads(i, carry):
        cc = pl.ds(al(i * nt, nt), nt)
        dyt = alls[1, :, cc].astype(F32)
        d_out = (gv_all[:, 0:1] * dyt).astype(BF)
        dwd[:, cc] = dot(tr[0], d_out).astype(BF)
        r = alls[0, :, cc]
        dwg[:, cc] = dot(tr[1], r).astype(BF)
        dwu[:, cc] = dot(tr[2], r).astype(BF)
        return carry

    lax.fori_loop(0, width // nt, grads, 0)
    stores = [
        pltpu.make_async_copy(v, h.at[0], loc.at[i])
        for i, (h, v) in enumerate(((dwg_h, dwg), (dwu_h, dwu), (dwd_h, dwd)))
    ]
    for c in stores:
        c.start()
    pltpu.make_async_copy(sc_part, sc_part, small_r.at[1]).wait()
    total = sc_p[mine, :]
    for j in range(1, 8):
        total += sc_r[j]
    score[0] = total.T[0:1]

    sub_r = lax.rem(lax.broadcasted_iota(jnp.int32, (tok_rows, nrow), 1) // SLOTS, SUB)
    tok_i = lax.broadcasted_iota(jnp.int32, (tok_rows, nrow), 0).astype(F32)
    tmatch = sidx_r == tok_i
    for c in range(RC):
        await_bytes(ret_r.at[c], r_recv.at[c])
        for b in range(SUB):
            hot = jnp.where(tmatch & (sub_r == b), 1.0, 0.0).astype(BF)
            col = (b // 2) * half + c * fw + (b % 2) * hw
            dtok[:, col : col + hw] = dot(hot, ret_r[c]).astype(BF)

    for wait in pending:
        wait()
    for c in stores:
        c.wait()


def on_device(tokens, cotangent, picks, gate_values, w_gate, w_up, w_down):
    tok_rows, width = tokens.shape
    experts = lax.axis_size("expert")
    groups = lax.axis_size("dp")
    ff = w_down.shape[1]
    cap = picks.shape[2]
    nrow = experts * ROWS
    half = width // 2
    cw = width // CH
    fw = half // RC
    rows = groups * cap
    vm = pl.BlockSpec(memory_space=pltpu.VMEM)
    hbm = pl.BlockSpec(memory_space=pl.ANY)
    dma = pltpu.SemaphoreType.DMA
    d_tokens, score, dwg, dwu, dwd = pl.pallas_call(
        functools.partial(kernel, experts),
        out_shape=(
            jax.ShapeDtypeStruct((tok_rows, width), BF),
            jax.ShapeDtypeStruct((1, 1, cap), F32),
            jax.ShapeDtypeStruct((1, ff, width), BF),
            jax.ShapeDtypeStruct((1, ff, width), BF),
            jax.ShapeDtypeStruct(w_down.shape, BF),
        ),
        in_specs=[vm] * 4 + [hbm] * 3,
        out_specs=[vm] * 2 + [hbm] * 3,
        scratch_shapes=[
            pltpu.VMEM((2 * CH, nrow, cw // SUB), BF),
            pltpu.VMEM((2 * CH, nrow, cw // SUB), BF),
            pltpu.VMEM((2, rows, width), BF),
            pltpu.VMEM((cap, 128), F32),
            pltpu.VMEM((rows, 128), F32),
            pltpu.VMEM((ff, width), BF),
            pltpu.VMEM((ff, width), BF),
            pltpu.VMEM((ff, width), BF),
            pltpu.VMEM((2, ff, half), BF),
            pltpu.VMEM((rows, ff), F32),
            pltpu.VMEM((rows, ff), F32),
            pltpu.VMEM((rows, ff), F32),
            pltpu.VMEM((2, rows, ff), BF),
            pltpu.VMEM((2, rows, ff), BF),
            pltpu.VMEM((3, ff, rows), BF),
            pltpu.VMEM((RC, 2, 2 * cap, fw // 2), BF),
            pltpu.VMEM((RC, 2, 2 * cap, fw // 2), BF),
            pltpu.VMEM((RC, 2, 2 * cap, fw), BF),
            pltpu.VMEM((RC, 2, 2 * cap, fw), BF),
            pltpu.VMEM((RC, 2 * cap, fw), BF),
            pltpu.VMEM((RC, cap, fw), BF),
            pltpu.VMEM((RC, nrow, fw // 2), BF),
            pltpu.VMEM((RC, nrow, fw // 2), BF),
            pltpu.VMEM((rows, 128), F32),
            pltpu.VMEM((groups, cap, 128), F32),
            pltpu.VMEM((ff, width), BF),
            pltpu.VMEM((ff, width), BF),
            pltpu.VMEM((ff, width), BF),
            dma((2 * CH,)), dma((2 * CH,)),
            dma((2 * CH, 9)), dma((2 * CH, 9)),
            dma((2,)), dma((2,)),
            dma((3,)), dma((3,)),
            dma((RC, 5)), dma((RC, 5)),
            dma((RC,)), dma((RC,)),
            dma((3,)),
        ],
        compiler_params=pltpu.CompilerParams(
            collective_id=0, has_side_effects=True, vmem_limit_bytes=58 * 2**20
        ),
        cost_estimate=pl.CostEstimate(
            flops=2 * 8 * rows * width * ff, bytes_accessed=12 * 2**20, transcendentals=rows * ff
        ),
    )(
        tokens, cotangent, picks, gate_values,
        jnp.swapaxes(w_gate, 1, 2), jnp.swapaxes(w_up, 1, 2), w_down,
    )
    return d_tokens, score, jnp.swapaxes(dwg, 1, 2), jnp.swapaxes(dwu, 1, 2), dwd


def solution(mesh):
    in_specs = (
        P(("dp", "expert"), None),
        P(("dp", "expert"), None),
        P("dp", None, None),
        P("dp", "expert", None),
        P("expert", None, "dp"),
        P("expert", None, "dp"),
        P("expert", "dp", None),
    )
    out_specs = (
        P(("dp", "expert"), None),
        P("dp", "expert", None),
        P("expert", None, "dp"),
        P("expert", None, "dp"),
        P("expert", "dp", None),
    )
    return jax.shard_map(
        on_device, mesh=mesh, in_specs=in_specs, out_specs=out_specs, check_vma=False
    )
```

```python
import functools

import jax
import jax.numpy as jnp
from jax import lax
from jax.experimental import pallas as pl
from jax.experimental.pallas import tpu as pltpu
from jax.sharding import PartitionSpec as P

MESH = pl.DeviceIdType.MESH
BF = jnp.bfloat16
F32 = jnp.float32
NT = (((1,), (1,)), ((), ()))
SLOTS = 4
SUB = 4
ROWS = SLOTS * SUB
CH = 2
RC = 4
PIECE = 64
DEPTH = 2


def dot(a, b):
    return jnp.dot(a, b, preferred_element_type=F32)


def dot_nt(a, b):
    return lax.dot_general(a, b, NT, preferred_element_type=F32)


def al(i, m):
    return pl.multiple_of(i, m)


def kernel(
    experts, tok, cot, picks, gates, wg_h, wu_h, wd_h,
    dtok, score, dwg_h, dwu_h, dwd_h,
    sendb, recvb, alls, gvb, gv_all, wg, wu, wd, wsib, gate, up, back, hid, dgu, dgs, tr,
    a_s, a_r, b_s, b_r, dg_own, dg_x, ret_s, ret_r, sc_p, sc_r, dwg, dwu, dwd,
    d_send, d_recv, g_send, g_recv, small_s, small_r, sib_s, sib_r, rs_s, rs_r, r_send, r_recv, loc,
):
    tok_rows, width = tok.shape
    cap = gvb.shape[0]
    dp = lax.axis_index("dp")
    ex = lax.axis_index("expert")
    y = dp // 2
    k = lax.rem(dp, 2)
    y_up, y_dn, y_op = lax.rem(y + 1, 4), lax.rem(y + 3, 4), lax.rem(y + 2, 4)
    up_d, dn_d, op_d, sib = y_up * 2 + k, y_dn * 2 + k, y_op * 2 + k, y * 2 + 1 - k
    half = width // 2
    cw = width // CH
    sw = cw // SUB
    nrow = experts * ROWS

    loads = [
        pltpu.make_async_copy(h.at[0], v, loc.at[i])
        for i, (h, v) in enumerate(((wg_h, wg), (wu_h, wu), (wd_h, wd)))
    ]
    for c in loads:
        c.start()

    pending = []
    barrier = pltpu.get_barrier_semaphore()

    def hail(d, carry):
        pl.semaphore_signal(
            barrier, inc=1, device_id=(dp, lax.rem(ex + d, experts)), device_id_type=MESH
        )
        return carry

    def hail_dp(d, carry):
        pl.semaphore_signal(
            barrier, inc=1, device_id=(lax.rem(dp + d, 8), ex), device_id_type=MESH
        )
        return carry

    lax.fori_loop(1, experts, hail, 0)
    lax.fori_loop(1, 8, hail_dp, 0)

    def copy(src, dst, s, r, to):
        return pltpu.make_async_remote_copy(
            src_ref=src, dst_ref=dst, send_sem=s, recv_sem=r, device_id=(to, ex), device_id_type=MESH
        )

    def push(src, dst, s, r, to):
        d = copy(src, dst, s, r, to)
        d.start()
        pending.append(d.wait_send)
        return d

    def spread(src, dst, s, r):
        def send(d, carry):
            to = lax.rem(ex + d, experts)
            pltpu.make_async_remote_copy(
                src_ref=src.at[pl.ds(al(to * ROWS, ROWS), ROWS)],
                dst_ref=dst.at[pl.ds(al(ex * ROWS, ROWS), ROWS)],
                send_sem=s, recv_sem=r, device_id=(dp, to), device_id_type=MESH,
            ).start()
            return carry

        lax.fori_loop(1, experts, send, 0)
        pending.append(lambda: await_bytes(src, s))

    def await_bytes(ref, sem):
        part = ref.at[pl.ds(0, nrow - ROWS)]
        pltpu.make_async_copy(part, part, sem).wait()

    shift = tok_rows.bit_length() - 1
    lists = picks[0]
    mine_f = jnp.where((lists >> shift) == ex, 1.0, 0.0)
    ahead = lax.broadcasted_iota(jnp.int32, (cap, cap), 0) < lax.broadcasted_iota(jnp.int32, (cap, cap), 1)
    place = dot(mine_f.astype(BF), jnp.where(ahead, 1.0, 0.0).astype(BF))
    token = ((lists & (tok_rows - 1)) + 1).astype(F32) * mine_f
    lane = lax.broadcasted_iota(jnp.int32, (experts, 128), 1)
    slots = jnp.zeros((experts, 128), F32)
    for s in range(SLOTS):
        at = jnp.sum(jnp.where(place == s, token, 0.0), axis=-1, keepdims=True)
        slots = jnp.where(lane == s, at, slots)
    grow = lax.broadcasted_iota(jnp.int32, (nrow, experts), 0) // ROWS
    spot = jnp.where(grow == lax.broadcasted_iota(jnp.int32, (nrow, experts), 1), 1.0, 0.0)
    spread_slots = dot(spot.astype(BF), slots.astype(BF))
    pick_lane = lax.rem(lax.broadcasted_iota(jnp.int32, (nrow, 128), 0), SLOTS)
    at_lane = lax.broadcasted_iota(jnp.int32, (nrow, 128), 1)
    sidx_c = jnp.sum(jnp.where(at_lane == pick_lane, spread_slots, 0.0), axis=-1, keepdims=True) - 1.0

    row_sub = lax.rem(lax.broadcasted_iota(jnp.int32, (nrow, tok_rows), 0) // SLOTS, SUB)
    col_tok = lax.broadcasted_iota(jnp.int32, (nrow, tok_rows), 1)
    match = sidx_c == col_tok.astype(F32)
    hots = [jnp.where(match & (row_sub == b), 1.0, 0.0).astype(BF) for b in range(SUB)]
    own = pl.ds(al(ex * ROWS, ROWS), ROWS)

    def dispatch(q):
        spread(sendb.at[q], recvb.at[q], d_send.at[q], d_recv.at[q])

    for q in range(2 * CH):
        src = tok if q < CH else cot
        base = (q % CH) * cw
        acc = dot(hots[0], src[:, base : base + sw])
        for b in range(1, SUB):
            acc += dot(hots[b], src[:, base + b * sw : base + (b + 1) * sw])
        sendb[q] = acc.astype(BF)
        recvb[q, own, :] = sendb[q, own, :]
        if q == 0:
            pl.semaphore_wait(barrier, experts - 1 + 7)
        if q < DEPTH:
            dispatch(q)

    own_row = picks[0, pl.ds(ex, 1), :]
    src_row = jnp.broadcast_to((own_row >> shift).astype(F32), (128, cap))
    src_col = src_row.T
    behind = lax.broadcasted_iota(jnp.int32, (cap, cap), 0) > lax.broadcasted_iota(jnp.int32, (cap, cap), 1)
    twins = jnp.where((src_col[:, :cap] == src_row[:cap]) & behind, 1.0, 0.0)
    rfl_c = src_col[:, 0:1] * ROWS + jnp.sum(twins, axis=-1, keepdims=True)
    rfl_r = jnp.broadcast_to(rfl_c, (cap, 128)).T[0:1]
    sidx_r = jnp.broadcast_to(sidx_c, (nrow, 128)).T[0:1]
    gvb[...] = jnp.broadcast_to(gates[0].astype(F32), (128, cap)).T

    mine = pl.ds(al(dp * cap, cap), cap)
    gv_all[mine, :] = gvb[...]

    def send_gv(d, carry):
        copy(gvb, gv_all.at[mine], small_s.at[0], small_r.at[0], lax.rem(dp + d, 8)).start()
        return carry

    lax.fori_loop(1, 8, send_gv, 0)
    gv_part = gv_all.at[pl.ds(0, 7 * cap)]
    pending.append(pltpu.make_async_copy(gv_part, gv_part, small_s.at[0]).wait)
    other = pl.ds(al((1 - k) * half, half), half)
    ws0 = push(wg_h.at[0, :, other], wsib.at[0], sib_s.at[0], sib_r.at[0], sib)
    ws1 = push(wu_h.at[0, :, other], wsib.at[1], sib_s.at[1], sib_r.at[1], sib)
    for c in loads:
        c.wait()

    lane_row = lax.broadcasted_iota(jnp.int32, (cap, nrow), 1).astype(F32)
    hc = cap // 2
    kt = 512
    hops = {}

    def blk(q, i, lo, n):
        return alls.at[q // CH, pl.ds(al(i * cap + lo, 16), n), pl.ds((q % CH) * cw, cw)]

    def pass_on(q, j, i, to, lo=0, n=cap):
        hops[q, j] = push(blk(q, i, lo, n), blk(q, i, lo, n), g_send.at[q, j], g_recv.at[q, j], to)

    def arrive(q):
        await_bytes(recvb.at[q], d_recv.at[q])
        for b in range(SUB):
            rhot = jnp.where(rfl_c + b * SLOTS == lane_row, 1.0, 0.0).astype(BF)
            col = (q % CH) * cw + b * sw
            alls[q // CH, mine, col : col + sw] = dot(rhot, recvb[q]).astype(BF)
        pass_on(q, 0, dp, up_d)
        pass_on(q, 1, dp, dn_d)
        pass_on(q, 2, dp, sib)
        if q + DEPTH < 2 * CH:
            dispatch(q + DEPTH)

    def forward(q):
        hops[q, 0].wait_recv()
        pass_on(q, 3, dn_d, up_d, 0, hc)
        pass_on(q, 4, dn_d, sib)
        hops[q, 1].wait_recv()
        pass_on(q, 5, up_d, dn_d, hc, hc)
        pass_on(q, 6, up_d, sib)

    def complete(q):
        hops[q, 3].wait_recv()
        pass_on(q, 7, op_d, sib, 0, hc)
        hops[q, 5].wait_recv()
        pass_on(q, 8, op_d, sib, hc, hc)
        for j in (2, 4, 6, 7, 8):
            hops[q, j].wait_recv()

    def products(q):
        c = q % CH

        def fwd(i, carry):
            kk = pl.ds(al(c * cw + i * kt, kt), kt)
            r = alls[0, :, kk]
            gate[...] += dot_nt(r, wg[:, kk])
            up[...] += dot_nt(r, wu[:, kk])
            return carry

        def bwd(i, carry):
            kk = pl.ds(al(c * cw + i * kt, kt), kt)
            back[...] += dot_nt(alls[1, :, kk], wd[:, kk])
            return carry

        lax.fori_loop(0, cw // kt, fwd if q < CH else bwd, 0)

    def activate(i, carry):
        r = pl.ds(al(i * 128, 128), 128)
        g, u = gate[r, :], up[r, :]
        s = jax.nn.sigmoid(g)
        act = g * s
        hid[r, :] = (act * u).astype(BF)
        gate[r, :] = u * s * (1.0 + g * (1.0 - s))
        up[r, :] = act
        return carry

    for acc in (gate, up, back):
        acc[...] = jnp.zeros_like(acc)
    for q in range(2 * CH):
        arrive(q)
        if q > 0:
            complete(q - 1)
            products(q - 1)
        forward(q)
        if q == CH:
            lax.fori_loop(0, 4, activate, 0)
    complete(2 * CH - 1)
    products(2 * CH - 1)

    pltpu.make_async_copy(gv_part, gv_part, small_r.at[0]).wait()

    def pointwise(i, carry):
        r = pl.ds(al(i * 128, 128), 128)
        dh = gv_all[r, 0:1] * back[r, :]
        dgu[0, r, :] = (dh * gate[r, :]).astype(BF)
        dgu[1, r, :] = (dh * up[r, :]).astype(BF)
        return carry

    lax.fori_loop(0, 4, pointwise, 0)
    dx = push(dgu, dgs, sib_s.at[2], sib_r.at[2], sib)

    two = 2 * cap
    fw = half // RC
    hw = fw // 2

    def part(yy, c, ready=()):
        r = pl.ds(al(yy * two, two), two)
        w_at = pl.ds(al(k * half + c * fw, fw), fw)
        o_at = pl.ds(c * fw, fw)
        t = dot(dgu[0, r, :], wg[:, w_at])
        t += dot(dgu[1, r, :], wu[:, w_at])
        for d in ready:
            d.wait_recv()
        t += dot(dgs[0, r, :], wsib[0, :, o_at])
        t += dot(dgs[1, r, :], wsib[1, :, o_at])
        return t

    a_cp, b_cp, x_cp = {}, {}, {}

    def far_terms(c):
        t = part(y_op, c, (ws0, ws1, dx) if c == 0 else ())
        a_s[c, 0] = t[:, :hw].astype(BF)
        a_s[c, 1] = t[:, hw:].astype(BF)
        for j, to in ((0, up_d), (1, dn_d)):
            a_cp[c, j] = push(a_s.at[c, j], a_r.at[c, j], rs_s.at[c, j], rs_r.at[c, j], to)

    def near_terms(c):
        for j, (yy, to) in enumerate(((y_up, up_d), (y_dn, dn_d))):
            t = part(yy, c)
            a_cp[c, j].wait_recv()
            at = slice(0, hw) if j == 0 else slice(hw, fw)
            rest = slice(hw, fw) if j == 0 else slice(0, hw)
            b_s[c, j, :, at] = (t[:, at] + a_r[c, j].astype(F32)).astype(BF)
            b_s[c, j, :, rest] = t[:, rest].astype(BF)
            b_cp[c, j] = push(b_s.at[c, j], b_r.at[c, j], rs_s.at[c, 2 + j], rs_r.at[c, 2 + j], to)

    def own_sum(c):
        t = part(y, c)
        b_cp[c, 0].wait_recv()
        b_cp[c, 1].wait_recv()
        t += b_r[c, 0].astype(F32) + b_r[c, 1].astype(F32)
        dg_own[c] = t.astype(BF)
        theirs = dg_own.at[c, pl.ds(al((1 - k) * cap, cap), cap)]
        x_cp[c] = push(theirs, dg_x.at[c], rs_s.at[c, 4], rs_r.at[c, 4], sib)

    row_i = lax.broadcasted_iota(jnp.int32, (nrow, cap), 0).astype(F32)

    def give_back(c):
        x_cp[c].wait_recv()
        mine_half = dg_own[c, pl.ds(al(k * cap, cap), cap), :]
        theirs = dg_x[c]
        h0 = jnp.where(k == 0, mine_half, theirs)
        h1 = jnp.where(k == 0, theirs, mine_half)
        acc = jnp.zeros((nrow, hw), F32)
        for b in range(SUB):
            hot = jnp.where(rfl_r + b * SLOTS == row_i, 1.0, 0.0).astype(BF)
            src = h0 if b < 2 else h1
            acc += dot(hot, src[:, (b % 2) * hw : (b % 2 + 1) * hw])
        ret_s[c] = acc.astype(BF)
        ret_r[c, own, :] = ret_s[c, own, :]
        spread(ret_s.at[c], ret_r.at[c], r_send.at[c], r_recv.at[c])

    far_terms(0)
    far_terms(1)
    near_terms(0)
    far_terms(2)
    near_terms(1)
    own_sum(0)
    for c in range(RC):
        if c + 3 < RC:
            far_terms(c + 3)
        if c + 2 < RC:
            near_terms(c + 2)
        if c + 1 < RC:
            own_sum(c + 1)
        give_back(c)

    def turn(i, carry):
        r = pl.ds(al(i * 128, 128), 128)
        hidden = hid[r, :].astype(F32)
        total = jnp.sum(hidden * back[r, :], axis=-1, keepdims=True)
        sc_p[r, :] = jnp.broadcast_to(total, (128, 128))
        tr[0, :, r] = hidden.T.astype(BF)
        tr[1, :, r] = dgu[0, r, :].astype(F32).T.astype(BF)
        tr[2, :, r] = dgu[1, r, :].astype(F32).T.astype(BF)
        return carry

    lax.fori_loop(0, 4, turn, 0)

    def send_score(d, carry):
        to = lax.rem(dp + d, 8)
        copy(
            sc_p.at[pl.ds(al(to * cap, cap), cap)], sc_r.at[lax.rem(8 - d, 8)],
            small_s.at[1], small_r.at[1], to,
        ).start()
        return carry

    lax.fori_loop(1, 8, send_score, 0)
    sc_part = sc_r.at[pl.ds(1, 7)]
    pending.append(pltpu.make_async_copy(sc_part, sc_part, small_s.at[1]).wait)

    nt = 512

    def grads(i, carry):
        cc = pl.ds(al(i * nt, nt), nt)
        dyt = alls[1, :, cc].astype(F32)
        d_out = (gv_all[:, 0:1] * dyt).astype(BF)
        dwd[:, cc] = dot(tr[0], d_out).astype(BF)
        r = alls[0, :, cc]
        dwg[:, cc] = dot(tr[1], r).astype(BF)
        dwu[:, cc] = dot(tr[2], r).astype(BF)
        return carry

    lax.fori_loop(0, width // nt, grads, 0)
    stores = [
        pltpu.make_async_copy(v, h.at[0], loc.at[i])
        for i, (h, v) in enumerate(((dwg_h, dwg), (dwu_h, dwu), (dwd_h, dwd)))
    ]
    for c in stores:
        c.start()
    pltpu.make_async_copy(sc_part, sc_part, small_r.at[1]).wait()
    total = sc_p[mine, :]
    for j in range(1, 8):
        total += sc_r[j]
    score[0] = total.T[0:1]

    sub_r = lax.rem(lax.broadcasted_iota(jnp.int32, (tok_rows, nrow), 1) // SLOTS, SUB)
    tok_i = lax.broadcasted_iota(jnp.int32, (tok_rows, nrow), 0).astype(F32)
    tmatch = sidx_r == tok_i
    for c in range(RC):
        await_bytes(ret_r.at[c], r_recv.at[c])
        for b in range(SUB):
            hot = jnp.where(tmatch & (sub_r == b), 1.0, 0.0).astype(BF)
            col = (b // 2) * half + c * fw + (b % 2) * hw
            dtok[:, col : col + hw] = dot(hot, ret_r[c]).astype(BF)

    for wait in pending:
        wait()
    for c in stores:
        c.wait()


def hand_over(*refs):
    n = (len(refs) - 2) // 3
    came, left = refs[-2], refs[-1]
    moves = []
    for i in range(n):
        src, dst, mid = refs[i], refs[n + i], refs[2 * n + i]
        rows = src.shape[-2]
        step = PIECE if rows % PIECE == 0 else rows
        for j in range(rows // step):
            at = (0,) * (len(src.shape) - 2) + (pl.ds(j * step, step),)
            moves.append((
                pltpu.make_async_copy(src.at[at], mid.at[at], came.at[i, j]),
                pltpu.make_async_copy(mid.at[at], dst.at[at], left.at[i, j]),
            ))
    for first, _ in moves:
        first.start()
    for first, second in moves:
        first.wait()
        second.start()
    for _, second in moves:
        second.wait()


def on_device(tokens, cotangent, picks, gate_values, w_gate, w_up, w_down):
    tok_rows, width = tokens.shape
    experts = lax.axis_size("expert")
    groups = lax.axis_size("dp")
    ff = w_down.shape[1]
    cap = picks.shape[2]
    nrow = experts * ROWS
    half = width // 2
    cw = width // CH
    fw = half // RC
    rows = groups * cap
    vm = pl.BlockSpec(memory_space=pltpu.VMEM)
    hbm = pl.BlockSpec(memory_space=pl.ANY)
    dma = pltpu.SemaphoreType.DMA
    results = pl.pallas_call(
        functools.partial(kernel, experts),
        out_shape=(
            jax.ShapeDtypeStruct((tok_rows, width), BF),
            jax.ShapeDtypeStruct((1, 1, cap), F32),
            jax.ShapeDtypeStruct((1, ff, width), BF),
            jax.ShapeDtypeStruct((1, ff, width), BF),
            jax.ShapeDtypeStruct(w_down.shape, BF),
        ),
        in_specs=[vm] * 4 + [hbm] * 3,
        out_specs=[vm] * 2 + [hbm] * 3,
        scratch_shapes=[
            pltpu.VMEM((2 * CH, nrow, cw // SUB), BF),
            pltpu.VMEM((2 * CH, nrow, cw // SUB), BF),
            pltpu.VMEM((2, rows, width), BF),
            pltpu.VMEM((cap, 128), F32),
            pltpu.VMEM((rows, 128), F32),
            pltpu.VMEM((ff, width), BF),
            pltpu.VMEM((ff, width), BF),
            pltpu.VMEM((ff, width), BF),
            pltpu.VMEM((2, ff, half), BF),
            pltpu.VMEM((rows, ff), F32),
            pltpu.VMEM((rows, ff), F32),
            pltpu.VMEM((rows, ff), F32),
            pltpu.VMEM((rows, ff), BF),
            pltpu.VMEM((2, rows, ff), BF),
            pltpu.VMEM((2, rows, ff), BF),
            pltpu.VMEM((3, ff, rows), BF),
            pltpu.VMEM((RC, 2, 2 * cap, fw // 2), BF),
            pltpu.VMEM((RC, 2, 2 * cap, fw // 2), BF),
            pltpu.VMEM((RC, 2, 2 * cap, fw), BF),
            pltpu.VMEM((RC, 2, 2 * cap, fw), BF),
            pltpu.VMEM((RC, 2 * cap, fw), BF),
            pltpu.VMEM((RC, cap, fw), BF),
            pltpu.VMEM((RC, nrow, fw // 2), BF),
            pltpu.VMEM((RC, nrow, fw // 2), BF),
            pltpu.VMEM((rows, 128), F32),
            pltpu.VMEM((groups, cap, 128), F32),
            pltpu.VMEM((ff, width), BF),
            pltpu.VMEM((ff, width), BF),
            pltpu.VMEM((ff, width), BF),
            dma((2 * CH,)), dma((2 * CH,)),
            dma((2 * CH, 9)), dma((2 * CH, 9)),
            dma((2,)), dma((2,)),
            dma((3,)), dma((3,)),
            dma((RC, 5)), dma((RC, 5)),
            dma((RC,)), dma((RC,)),
            dma((3,)),
        ],
        compiler_params=pltpu.CompilerParams(
            collective_id=0, has_side_effects=True, vmem_limit_bytes=58 * 2**20
        ),
        cost_estimate=pl.CostEstimate(
            flops=2 * 8 * rows * width * ff, bytes_accessed=12 * 2**20, transcendentals=rows * ff
        ),
    )(
        tokens, cotangent, picks, gate_values,
        jnp.swapaxes(w_gate, 1, 2), jnp.swapaxes(w_up, 1, 2), w_down,
    )
    d_tokens, score, dwg, dwu, dwd = pl.pallas_call(
        hand_over,
        out_shape=[jax.ShapeDtypeStruct(r.shape, r.dtype) for r in results],
        in_specs=[hbm] * 5,
        out_specs=[hbm] * 5,
        scratch_shapes=[pltpu.VMEM(r.shape, r.dtype) for r in results] + [dma((5, 4)), dma((5, 4))],
    )(*results)
    return d_tokens, score, jnp.swapaxes(dwg, 1, 2), jnp.swapaxes(dwu, 1, 2), dwd


def solution(mesh):
    in_specs = (
        P(("dp", "expert"), None),
        P(("dp", "expert"), None),
        P("dp", None, None),
        P("dp", "expert", None),
        P("expert", None, "dp"),
        P("expert", None, "dp"),
        P("expert", "dp", None),
    )
    out_specs = (
        P(("dp", "expert"), None),
        P("dp", "expert", None),
        P("expert", None, "dp"),
        P("expert", None, "dp"),
        P("expert", "dp", None),
    )
    return jax.shard_map(
        on_device, mesh=mesh, in_specs=in_specs, out_specs=out_specs, check_vma=False
    )
```

```python
import functools

import jax
import jax.numpy as jnp
from jax import lax
from jax.experimental import pallas as pl
from jax.experimental.pallas import tpu as pltpu
from jax.sharding import PartitionSpec as P

MESH = pl.DeviceIdType.MESH
BF = jnp.bfloat16
F32 = jnp.float32
NT = (((1,), (1,)), ((), ()))
SLOTS = 4
SUB = 4
ROWS = SLOTS * SUB
CH = 2
RC = 4
PIECE = 64
DEPTH = 2


def dot(a, b):
    return jnp.dot(a, b, preferred_element_type=F32)


def dot_nt(a, b):
    return lax.dot_general(a, b, NT, preferred_element_type=F32)


def al(i, m):
    return pl.multiple_of(i, m)


def kernel(
    experts, tok, cot, picks, gates, wg_h, wu_h, wd_h,
    dtok, score, dwg_h, dwu_h, dwd_h,
    gcat, ccat, bcat, fcat, sendb, recvb, alls, gvb, gv_all, wg, wu, wd, wsib, gate, up, back, hid, dgu, dgs, tr,
    a_s, a_r, b_s, b_r, dg_own, dg_x, ret_s, ret_r, sc_p, sc_r, dwg, dwu, dwd,
    d_send, d_recv, g_send, g_recv, small_s, small_r, sib_s, sib_r, rs_s, rs_r, r_send, r_recv, loc,
):
    tok_rows, width = tok.shape
    cap = gvb.shape[0]
    dp = lax.axis_index("dp")
    ex = lax.axis_index("expert")
    y = dp // 2
    k = lax.rem(dp, 2)
    y_up, y_dn, y_op = lax.rem(y + 1, 4), lax.rem(y + 3, 4), lax.rem(y + 2, 4)
    up_d, dn_d, op_d, sib = y_up * 2 + k, y_dn * 2 + k, y_op * 2 + k, y * 2 + 1 - k
    half = width // 2
    cw = width // CH
    sw = cw // SUB
    nrow = experts * ROWS

    loads = [
        pltpu.make_async_copy(h.at[0], v, loc.at[i])
        for i, (h, v) in enumerate(((wg_h, wg), (wu_h, wu), (wd_h, wd)))
    ]
    for c in loads:
        c.start()

    pending = []
    barrier = pltpu.get_barrier_semaphore()

    def hail(d, carry):
        pl.semaphore_signal(
            barrier, inc=1, device_id=(dp, lax.rem(ex + d, experts)), device_id_type=MESH
        )
        return carry

    def hail_dp(d, carry):
        pl.semaphore_signal(
            barrier, inc=1, device_id=(lax.rem(dp + d, 8), ex), device_id_type=MESH
        )
        return carry

    lax.fori_loop(1, experts, hail, 0)
    lax.fori_loop(1, 8, hail_dp, 0)

    def copy(src, dst, s, r, to):
        return pltpu.make_async_remote_copy(
            src_ref=src, dst_ref=dst, send_sem=s, recv_sem=r, device_id=(to, ex), device_id_type=MESH
        )

    def push(src, dst, s, r, to):
        d = copy(src, dst, s, r, to)
        d.start()
        pending.append(d.wait_send)
        return d

    def spread(src, dst, s, r):
        def send(d, carry):
            to = lax.rem(ex + d, experts)
            pltpu.make_async_remote_copy(
                src_ref=src.at[pl.ds(al(to * ROWS, ROWS), ROWS)],
                dst_ref=dst.at[pl.ds(al(ex * ROWS, ROWS), ROWS)],
                send_sem=s, recv_sem=r, device_id=(dp, to), device_id_type=MESH,
            ).start()
            return carry

        lax.fori_loop(1, experts, send, 0)
        pending.append(lambda: await_bytes(src, s))

    def await_bytes(ref, sem):
        part = ref.at[pl.ds(0, nrow - ROWS)]
        pltpu.make_async_copy(part, part, sem).wait()

    shift = tok_rows.bit_length() - 1
    lists = picks[0]
    mine_f = jnp.where((lists >> shift) == ex, 1.0, 0.0)
    ahead = lax.broadcasted_iota(jnp.int32, (cap, cap), 0) < lax.broadcasted_iota(jnp.int32, (cap, cap), 1)
    place = dot(mine_f.astype(BF), jnp.where(ahead, 1.0, 0.0).astype(BF))
    token = ((lists & (tok_rows - 1)) + 1).astype(F32) * mine_f
    lane = lax.broadcasted_iota(jnp.int32, (experts, 128), 1)
    slots = jnp.zeros((experts, 128), F32)
    for s in range(SLOTS):
        at = jnp.sum(jnp.where(place == s, token, 0.0), axis=-1, keepdims=True)
        slots = jnp.where(lane == s, at, slots)
    grow = lax.broadcasted_iota(jnp.int32, (nrow, experts), 0) // ROWS
    spot = jnp.where(grow == lax.broadcasted_iota(jnp.int32, (nrow, experts), 1), 1.0, 0.0)
    spread_slots = dot(spot.astype(BF), slots.astype(BF))
    pick_lane = lax.rem(lax.broadcasted_iota(jnp.int32, (nrow, 128), 0), SLOTS)
    at_lane = lax.broadcasted_iota(jnp.int32, (nrow, 128), 1)
    sidx_c = jnp.sum(jnp.where(at_lane == pick_lane, spread_slots, 0.0), axis=-1, keepdims=True) - 1.0

    row_sub = lax.rem(lax.broadcasted_iota(jnp.int32, (nrow, tok_rows), 0) // SLOTS, SUB)
    col_tok = lax.broadcasted_iota(jnp.int32, (nrow, tok_rows), 1)
    match = sidx_c == col_tok.astype(F32)
    for b in range(SUB):
        gcat[:, b * tok_rows : (b + 1) * tok_rows] = jnp.where(match & (row_sub == b), 1.0, 0.0).astype(BF)
    own = pl.ds(al(ex * ROWS, ROWS), ROWS)

    def dispatch(q):
        spread(sendb.at[q], recvb.at[q], d_send.at[q], d_recv.at[q])

    for q in range(2 * CH):
        src = tok if q < CH else cot
        base = (q % CH) * cw
        stacked = jnp.concatenate([src[:, base + b * sw : base + (b + 1) * sw] for b in range(SUB)], axis=0)
        sendb[q] = dot(gcat[...], stacked).astype(BF)
        recvb[q, own, :] = sendb[q, own, :]
        if q == 0:
            pl.semaphore_wait(barrier, experts - 1 + 7)
        if q < DEPTH:
            dispatch(q)

    own_row = picks[0, pl.ds(ex, 1), :]
    src_row = jnp.broadcast_to((own_row >> shift).astype(F32), (128, cap))
    src_col = src_row.T
    behind = lax.broadcasted_iota(jnp.int32, (cap, cap), 0) > lax.broadcasted_iota(jnp.int32, (cap, cap), 1)
    twins = jnp.where((src_col[:, :cap] == src_row[:cap]) & behind, 1.0, 0.0)
    rfl_c = src_col[:, 0:1] * ROWS + jnp.sum(twins, axis=-1, keepdims=True)
    at_c = jnp.concatenate([rfl_c + b * SLOTS for b in range(SUB)], axis=0)
    at_r = jnp.broadcast_to(at_c, (SUB * cap, 128)).T[0:1]
    sidx_r = jnp.broadcast_to(sidx_c, (nrow, 128)).T[0:1]
    gvb[...] = jnp.broadcast_to(gates[0].astype(F32), (128, cap)).T

    mine = pl.ds(al(dp * cap, cap), cap)
    gv_all[mine, :] = gvb[...]

    def send_gv(d, carry):
        copy(gvb, gv_all.at[mine], small_s.at[0], small_r.at[0], lax.rem(dp + d, 8)).start()
        return carry

    lax.fori_loop(1, 8, send_gv, 0)
    gv_part = gv_all.at[pl.ds(0, 7 * cap)]
    pending.append(pltpu.make_async_copy(gv_part, gv_part, small_s.at[0]).wait)
    other = pl.ds(al((1 - k) * half, half), half)
    ws0 = push(wg_h.at[0, :, other], wsib.at[0], sib_s.at[0], sib_r.at[0], sib)
    ws1 = push(wu_h.at[0, :, other], wsib.at[1], sib_s.at[1], sib_r.at[1], sib)
    for c in loads:
        c.wait()

    lane_row = lax.broadcasted_iota(jnp.int32, (SUB * cap, nrow), 1).astype(F32)
    ccat[...] = jnp.where(at_c == lane_row, 1.0, 0.0).astype(BF)
    row_i = lax.broadcasted_iota(jnp.int32, (nrow, SUB * cap), 0).astype(F32)
    bcat[...] = jnp.where(at_r == row_i, 1.0, 0.0).astype(BF)
    sub_r = lax.rem(lax.broadcasted_iota(jnp.int32, (tok_rows, nrow), 1) // SLOTS, SUB)
    tok_i = lax.broadcasted_iota(jnp.int32, (tok_rows, nrow), 0).astype(F32)
    tmatch = sidx_r == tok_i
    for b in range(SUB):
        fcat[b * tok_rows : (b + 1) * tok_rows, :] = jnp.where(tmatch & (sub_r == b), 1.0, 0.0).astype(BF)

    hc = cap // 2
    kt = 512
    hops = {}

    def blk(q, i, lo, n):
        return alls.at[q // CH, pl.ds(al(i * cap + lo, 16), n), pl.ds((q % CH) * cw, cw)]

    def pass_on(q, j, i, to, lo=0, n=cap):
        hops[q, j] = push(blk(q, i, lo, n), blk(q, i, lo, n), g_send.at[q, j], g_recv.at[q, j], to)

    def arrive(q):
        await_bytes(recvb.at[q], d_recv.at[q])
        packed = dot(ccat[...], recvb[q]).astype(BF)
        for b in range(SUB):
            col = (q % CH) * cw + b * sw
            alls[q // CH, mine, col : col + sw] = packed[b * cap : (b + 1) * cap]
        pass_on(q, 0, dp, up_d)
        pass_on(q, 1, dp, dn_d)
        pass_on(q, 2, dp, sib)
        if q + DEPTH < 2 * CH:
            dispatch(q + DEPTH)

    def forward(q):
        hops[q, 0].wait_recv()
        pass_on(q, 3, dn_d, up_d, 0, hc)
        pass_on(q, 4, dn_d, sib)
        hops[q, 1].wait_recv()
        pass_on(q, 5, up_d, dn_d, hc, hc)
        pass_on(q, 6, up_d, sib)

    def complete(q):
        hops[q, 3].wait_recv()
        pass_on(q, 7, op_d, sib, 0, hc)
        hops[q, 5].wait_recv()
        pass_on(q, 8, op_d, sib, hc, hc)
        for j in (2, 4, 6, 7, 8):
            hops[q, j].wait_recv()

    def products(q):
        c = q % CH

        def fwd(i, carry):
            kk = pl.ds(al(c * cw + i * kt, kt), kt)
            r = alls[0, :, kk]
            gate[...] += dot_nt(r, wg[:, kk])
            up[...] += dot_nt(r, wu[:, kk])
            return carry

        def bwd(i, carry):
            kk = pl.ds(al(c * cw + i * kt, kt), kt)
            back[...] += dot_nt(alls[1, :, kk], wd[:, kk])
            return carry

        lax.fori_loop(0, cw // kt, fwd if q < CH else bwd, 0)

    def activate(i, carry):
        r = pl.ds(al(i * 128, 128), 128)
        g, u = gate[r, :], up[r, :]
        s = jax.nn.sigmoid(g)
        act = g * s
        hid[r, :] = (act * u).astype(BF)
        gate[r, :] = u * s * (1.0 + g * (1.0 - s))
        up[r, :] = act
        return carry

    for acc in (gate, up, back):
        acc[...] = jnp.zeros_like(acc)
    for q in range(2 * CH):
        arrive(q)
        if q > 0:
            complete(q - 1)
            products(q - 1)
        forward(q)
        if q == CH:
            lax.fori_loop(0, 4, activate, 0)
    complete(2 * CH - 1)
    products(2 * CH - 1)

    pltpu.make_async_copy(gv_part, gv_part, small_r.at[0]).wait()

    def pointwise(i, carry):
        r = pl.ds(al(i * 128, 128), 128)
        dh = gv_all[r, 0:1] * back[r, :]
        dgu[0, r, :] = (dh * gate[r, :]).astype(BF)
        dgu[1, r, :] = (dh * up[r, :]).astype(BF)
        return carry

    lax.fori_loop(0, 4, pointwise, 0)
    dx = push(dgu, dgs, sib_s.at[2], sib_r.at[2], sib)

    two = 2 * cap
    fw = half // RC
    hw = fw // 2

    def part(yy, c, ready=()):
        r = pl.ds(al(yy * two, two), two)
        w_at = pl.ds(al(k * half + c * fw, fw), fw)
        o_at = pl.ds(c * fw, fw)
        t = dot(dgu[0, r, :], wg[:, w_at])
        t += dot(dgu[1, r, :], wu[:, w_at])
        for d in ready:
            d.wait_recv()
        t += dot(dgs[0, r, :], wsib[0, :, o_at])
        t += dot(dgs[1, r, :], wsib[1, :, o_at])
        return t

    a_cp, b_cp, x_cp = {}, {}, {}

    def far_terms(c):
        t = part(y_op, c, (ws0, ws1, dx) if c == 0 else ())
        a_s[c, 0] = t[:, :hw].astype(BF)
        a_s[c, 1] = t[:, hw:].astype(BF)
        for j, to in ((0, up_d), (1, dn_d)):
            a_cp[c, j] = push(a_s.at[c, j], a_r.at[c, j], rs_s.at[c, j], rs_r.at[c, j], to)

    def near_terms(c):
        for j, (yy, to) in enumerate(((y_up, up_d), (y_dn, dn_d))):
            t = part(yy, c)
            a_cp[c, j].wait_recv()
            at = slice(0, hw) if j == 0 else slice(hw, fw)
            rest = slice(hw, fw) if j == 0 else slice(0, hw)
            b_s[c, j, :, at] = (t[:, at] + a_r[c, j].astype(F32)).astype(BF)
            b_s[c, j, :, rest] = t[:, rest].astype(BF)
            b_cp[c, j] = push(b_s.at[c, j], b_r.at[c, j], rs_s.at[c, 2 + j], rs_r.at[c, 2 + j], to)

    def own_sum(c):
        t = part(y, c)
        b_cp[c, 0].wait_recv()
        b_cp[c, 1].wait_recv()
        t += b_r[c, 0].astype(F32) + b_r[c, 1].astype(F32)
        dg_own[c] = t.astype(BF)
        theirs = dg_own.at[c, pl.ds(al((1 - k) * cap, cap), cap)]
        x_cp[c] = push(theirs, dg_x.at[c], rs_s.at[c, 4], rs_r.at[c, 4], sib)

    def give_back(c):
        x_cp[c].wait_recv()
        mine_half = dg_own[c, pl.ds(al(k * cap, cap), cap), :]
        theirs = dg_x[c]
        h0 = jnp.where(k == 0, mine_half, theirs)
        h1 = jnp.where(k == 0, theirs, mine_half)
        stacked = jnp.concatenate([h0[:, :hw], h0[:, hw:], h1[:, :hw], h1[:, hw:]], axis=0)
        ret_s[c] = dot(bcat[...], stacked).astype(BF)
        ret_r[c, own, :] = ret_s[c, own, :]
        spread(ret_s.at[c], ret_r.at[c], r_send.at[c], r_recv.at[c])

    far_terms(0)
    far_terms(1)
    near_terms(0)
    far_terms(2)
    near_terms(1)
    own_sum(0)
    for c in range(RC):
        if c + 3 < RC:
            far_terms(c + 3)
        if c + 2 < RC:
            near_terms(c + 2)
        if c + 1 < RC:
            own_sum(c + 1)
        give_back(c)

    def turn(i, carry):
        r = pl.ds(al(i * 128, 128), 128)
        hidden = hid[r, :].astype(F32)
        total = jnp.sum(hidden * back[r, :], axis=-1, keepdims=True)
        sc_p[r, :] = jnp.broadcast_to(total, (128, 128))
        tr[0, :, r] = hidden.T.astype(BF)
        tr[1, :, r] = dgu[0, r, :].astype(F32).T.astype(BF)
        tr[2, :, r] = dgu[1, r, :].astype(F32).T.astype(BF)
        return carry

    lax.fori_loop(0, 4, turn, 0)

    def send_score(d, carry):
        to = lax.rem(dp + d, 8)
        copy(
            sc_p.at[pl.ds(al(to * cap, cap), cap)], sc_r.at[lax.rem(8 - d, 8)],
            small_s.at[1], small_r.at[1], to,
        ).start()
        return carry

    lax.fori_loop(1, 8, send_score, 0)
    sc_part = sc_r.at[pl.ds(1, 7)]
    pending.append(pltpu.make_async_copy(sc_part, sc_part, small_s.at[1]).wait)

    nt = 512

    def grads(i, carry):
        cc = pl.ds(al(i * nt, nt), nt)
        dyt = alls[1, :, cc].astype(F32)
        d_out = (gv_all[:, 0:1] * dyt).astype(BF)
        dwd[:, cc] = dot(tr[0], d_out).astype(BF)
        r = alls[0, :, cc]
        dwg[:, cc] = dot(tr[1], r).astype(BF)
        dwu[:, cc] = dot(tr[2], r).astype(BF)
        return carry

    lax.fori_loop(0, width // nt, grads, 0)
    stores = [
        pltpu.make_async_copy(v, h.at[0], loc.at[i])
        for i, (h, v) in enumerate(((dwg_h, dwg), (dwu_h, dwu), (dwd_h, dwd)))
    ]
    for c in stores:
        c.start()
    pltpu.make_async_copy(sc_part, sc_part, small_r.at[1]).wait()
    total = sc_p[mine, :]
    for j in range(1, 8):
        total += sc_r[j]
    score[0] = total.T[0:1]

    for c in range(RC):
        await_bytes(ret_r.at[c], r_recv.at[c])
        sums = dot(fcat[...], ret_r[c]).astype(BF)
        for b in range(SUB):
            col = (b // 2) * half + c * fw + (b % 2) * hw
            dtok[:, col : col + hw] = sums[b * tok_rows : (b + 1) * tok_rows]

    for wait in pending:
        wait()
    for c in stores:
        c.wait()


def hand_over(*refs):
    n = (len(refs) - 2) // 3
    came, left = refs[-2], refs[-1]
    moves = []
    for i in range(n):
        src, dst, mid = refs[i], refs[n + i], refs[2 * n + i]
        rows = src.shape[-2]
        step = PIECE if rows % PIECE == 0 else rows
        for j in range(rows // step):
            at = (0,) * (len(src.shape) - 2) + (pl.ds(j * step, step),)
            moves.append((
                pltpu.make_async_copy(src.at[at], mid.at[at], came.at[i, j]),
                pltpu.make_async_copy(mid.at[at], dst.at[at], left.at[i, j]),
            ))
    for first, _ in moves:
        first.start()
    for first, second in moves:
        first.wait()
        second.start()
    for _, second in moves:
        second.wait()


def on_device(tokens, cotangent, picks, gate_values, w_gate, w_up, w_down):
    tok_rows, width = tokens.shape
    experts = lax.axis_size("expert")
    groups = lax.axis_size("dp")
    ff = w_down.shape[1]
    cap = picks.shape[2]
    nrow = experts * ROWS
    half = width // 2
    cw = width // CH
    fw = half // RC
    rows = groups * cap
    vm = pl.BlockSpec(memory_space=pltpu.VMEM)
    hbm = pl.BlockSpec(memory_space=pl.ANY)
    dma = pltpu.SemaphoreType.DMA
    results = pl.pallas_call(
        functools.partial(kernel, experts),
        out_shape=(
            jax.ShapeDtypeStruct((tok_rows, width), BF),
            jax.ShapeDtypeStruct((1, 1, cap), F32),
            jax.ShapeDtypeStruct((1, ff, width), BF),
            jax.ShapeDtypeStruct((1, ff, width), BF),
            jax.ShapeDtypeStruct(w_down.shape, BF),
        ),
        in_specs=[vm] * 4 + [hbm] * 3,
        out_specs=[vm] * 2 + [hbm] * 3,
        scratch_shapes=[
            pltpu.VMEM((nrow, SUB * tok_rows), BF),
            pltpu.VMEM((SUB * cap, nrow), BF),
            pltpu.VMEM((nrow, SUB * cap), BF),
            pltpu.VMEM((SUB * tok_rows, nrow), BF),
            pltpu.VMEM((2 * CH, nrow, cw // SUB), BF),
            pltpu.VMEM((2 * CH, nrow, cw // SUB), BF),
            pltpu.VMEM((2, rows, width), BF),
            pltpu.VMEM((cap, 128), F32),
            pltpu.VMEM((rows, 128), F32),
            pltpu.VMEM((ff, width), BF),
            pltpu.VMEM((ff, width), BF),
            pltpu.VMEM((ff, width), BF),
            pltpu.VMEM((2, ff, half), BF),
            pltpu.VMEM((rows, ff), F32),
            pltpu.VMEM((rows, ff), F32),
            pltpu.VMEM((rows, ff), F32),
            pltpu.VMEM((rows, ff), BF),
            pltpu.VMEM((2, rows, ff), BF),
            pltpu.VMEM((2, rows, ff), BF),
            pltpu.VMEM((3, ff, rows), BF),
            pltpu.VMEM((RC, 2, 2 * cap, fw // 2), BF),
            pltpu.VMEM((RC, 2, 2 * cap, fw // 2), BF),
            pltpu.VMEM((RC, 2, 2 * cap, fw), BF),
            pltpu.VMEM((RC, 2, 2 * cap, fw), BF),
            pltpu.VMEM((RC, 2 * cap, fw), BF),
            pltpu.VMEM((RC, cap, fw), BF),
            pltpu.VMEM((RC, nrow, fw // 2), BF),
            pltpu.VMEM((RC, nrow, fw // 2), BF),
            pltpu.VMEM((rows, 128), F32),
            pltpu.VMEM((groups, cap, 128), F32),
            pltpu.VMEM((ff, width), BF),
            pltpu.VMEM((ff, width), BF),
            pltpu.VMEM((ff, width), BF),
            dma((2 * CH,)), dma((2 * CH,)),
            dma((2 * CH, 9)), dma((2 * CH, 9)),
            dma((2,)), dma((2,)),
            dma((3,)), dma((3,)),
            dma((RC, 5)), dma((RC, 5)),
            dma((RC,)), dma((RC,)),
            dma((3,)),
        ],
        compiler_params=pltpu.CompilerParams(
            collective_id=0, has_side_effects=True, vmem_limit_bytes=58 * 2**20
        ),
        cost_estimate=pl.CostEstimate(
            flops=2 * 8 * rows * width * ff, bytes_accessed=12 * 2**20, transcendentals=rows * ff
        ),
    )(
        tokens, cotangent, picks, gate_values,
        jnp.swapaxes(w_gate, 1, 2), jnp.swapaxes(w_up, 1, 2), w_down,
    )
    d_tokens, score, dwg, dwu, dwd = pl.pallas_call(
        hand_over,
        out_shape=[jax.ShapeDtypeStruct(r.shape, r.dtype) for r in results],
        in_specs=[hbm] * 5,
        out_specs=[hbm] * 5,
        scratch_shapes=[pltpu.VMEM(r.shape, r.dtype) for r in results] + [dma((5, 4)), dma((5, 4))],
    )(*results)
    return d_tokens, score, jnp.swapaxes(dwg, 1, 2), jnp.swapaxes(dwu, 1, 2), dwd


def solution(mesh):
    in_specs = (
        P(("dp", "expert"), None),
        P(("dp", "expert"), None),
        P("dp", None, None),
        P("dp", "expert", None),
        P("expert", None, "dp"),
        P("expert", None, "dp"),
        P("expert", "dp", None),
    )
    out_specs = (
        P(("dp", "expert"), None),
        P("dp", "expert", None),
        P("expert", None, "dp"),
        P("expert", None, "dp"),
        P("expert", "dp", None),
    )
    return jax.shard_map(
        on_device, mesh=mesh, in_specs=in_specs, out_specs=out_specs, check_vma=False
    )
```

```python
import functools

import jax
import jax.numpy as jnp
from jax import lax
from jax.experimental import pallas as pl
from jax.experimental.pallas import tpu as pltpu
from jax.sharding import PartitionSpec as P

MESH = pl.DeviceIdType.MESH
BF = jnp.bfloat16
F32 = jnp.float32
NT = (((1,), (1,)), ((), ()))
SLOTS = 4
SUB = 4
ROWS = SLOTS * SUB
CH = 2
RC = 4
PIECE = 64
DEPTH = 2


def dot(a, b):
    return jnp.dot(a, b, preferred_element_type=F32)


def dot_nt(a, b):
    return lax.dot_general(a, b, NT, preferred_element_type=F32)


def al(i, m):
    return pl.multiple_of(i, m)


def kernel(
    experts, tok, cot, picks, gates, wg_h, wu_h, wd_h,
    dtok, score, dwg_h, dwu_h, dwd_h,
    gcat, ccat, bcat, fcat, sendb, recvb, alls, gvb, gv_all, wg, wu, wd, wsib, gate, up, back, hid, dgu, dgs, tr,
    a_s, a_r, b_s, b_r, dg_own, dg_x, ret_s, ret_r, sc_p, sc_r, dwg, dwu, dwd,
    d_send, d_recv, g_send, g_recv, small_s, small_r, sib_s, sib_r, rs_s, rs_r, r_send, r_recv, loc,
):
    tok_rows, width = tok.shape
    cap = gvb.shape[0]
    dp = lax.axis_index("dp")
    ex = lax.axis_index("expert")
    y = dp // 2
    k = lax.rem(dp, 2)
    y_up, y_dn, y_op = lax.rem(y + 1, 4), lax.rem(y + 3, 4), lax.rem(y + 2, 4)
    up_d, dn_d, op_d, sib = y_up * 2 + k, y_dn * 2 + k, y_op * 2 + k, y * 2 + 1 - k
    half = width // 2
    cw = width // CH
    sw = cw // SUB
    nrow = experts * ROWS

    loads = [
        pltpu.make_async_copy(h.at[0], v, loc.at[i])
        for i, (h, v) in enumerate(((wg_h, wg), (wu_h, wu), (wd_h, wd)))
    ]
    for c in loads:
        c.start()

    pending = []
    barrier = pltpu.get_barrier_semaphore()

    def hail(d, carry):
        pl.semaphore_signal(
            barrier, inc=1, device_id=(dp, lax.rem(ex + d, experts)), device_id_type=MESH
        )
        return carry

    def hail_dp(d, carry):
        pl.semaphore_signal(
            barrier, inc=1, device_id=(lax.rem(dp + d, 8), ex), device_id_type=MESH
        )
        return carry

    lax.fori_loop(1, experts, hail, 0)
    lax.fori_loop(1, 8, hail_dp, 0)

    def copy(src, dst, s, r, to):
        return pltpu.make_async_remote_copy(
            src_ref=src, dst_ref=dst, send_sem=s, recv_sem=r, device_id=(to, ex), device_id_type=MESH
        )

    def push(src, dst, s, r, to):
        d = copy(src, dst, s, r, to)
        d.start()
        pending.append(d.wait_send)
        return d

    def spread(src, dst, s, r):
        def send(d, carry):
            to = lax.rem(ex + d, experts)
            pltpu.make_async_remote_copy(
                src_ref=src.at[pl.ds(al(to * ROWS, ROWS), ROWS)],
                dst_ref=dst.at[pl.ds(al(ex * ROWS, ROWS), ROWS)],
                send_sem=s, recv_sem=r, device_id=(dp, to), device_id_type=MESH,
            ).start()
            return carry

        lax.fori_loop(1, experts, send, 0)
        pending.append(lambda: await_bytes(src, s))

    def await_bytes(ref, sem):
        part = ref.at[pl.ds(0, nrow - ROWS)]
        pltpu.make_async_copy(part, part, sem).wait()

    shift = tok_rows.bit_length() - 1
    lists = picks[0]
    mine_f = jnp.where((lists >> shift) == ex, 1.0, 0.0)
    ahead = lax.broadcasted_iota(jnp.int32, (cap, cap), 0) < lax.broadcasted_iota(jnp.int32, (cap, cap), 1)
    place = dot(mine_f.astype(BF), jnp.where(ahead, 1.0, 0.0).astype(BF))
    token = ((lists & (tok_rows - 1)) + 1).astype(F32) * mine_f
    lane = lax.broadcasted_iota(jnp.int32, (experts, 128), 1)
    slots = jnp.zeros((experts, 128), F32)
    for s in range(SLOTS):
        at = jnp.sum(jnp.where(place == s, token, 0.0), axis=-1, keepdims=True)
        slots = jnp.where(lane == s, at, slots)
    grow = lax.broadcasted_iota(jnp.int32, (nrow, experts), 0) // ROWS
    spot = jnp.where(grow == lax.broadcasted_iota(jnp.int32, (nrow, experts), 1), 1.0, 0.0)
    spread_slots = dot(spot.astype(BF), slots.astype(BF))
    pick_lane = lax.rem(lax.broadcasted_iota(jnp.int32, (nrow, 128), 0), SLOTS)
    at_lane = lax.broadcasted_iota(jnp.int32, (nrow, 128), 1)
    sidx_c = jnp.sum(jnp.where(at_lane == pick_lane, spread_slots, 0.0), axis=-1, keepdims=True) - 1.0

    row_sub = lax.rem(lax.broadcasted_iota(jnp.int32, (nrow, tok_rows), 0) // SLOTS, SUB)
    col_tok = lax.broadcasted_iota(jnp.int32, (nrow, tok_rows), 1)
    match = sidx_c == col_tok.astype(F32)
    for b in range(SUB):
        gcat[:, b * tok_rows : (b + 1) * tok_rows] = jnp.where(match & (row_sub == b), 1.0, 0.0).astype(BF)
    own = pl.ds(al(ex * ROWS, ROWS), ROWS)

    def dispatch(q):
        spread(sendb.at[q], recvb.at[q], d_send.at[q], d_recv.at[q])

    for q in range(2 * CH):
        src = tok if q < CH else cot
        base = (q % CH) * cw
        stacked = jnp.concatenate([src[:, base + b * sw : base + (b + 1) * sw] for b in range(SUB)], axis=0)
        sendb[q] = dot(gcat[...], stacked).astype(BF)
        recvb[q, own, :] = sendb[q, own, :]
        if q == 0:
            pl.semaphore_wait(barrier, experts - 1 + 7)
        if q < DEPTH:
            dispatch(q)

    own_row = picks[0, pl.ds(ex, 1), :]
    src_row = jnp.broadcast_to((own_row >> shift).astype(F32), (128, cap))
    src_col = src_row.T
    behind = lax.broadcasted_iota(jnp.int32, (cap, cap), 0) > lax.broadcasted_iota(jnp.int32, (cap, cap), 1)
    twins = jnp.where((src_col[:, :cap] == src_row[:cap]) & behind, 1.0, 0.0)
    rfl_c = src_col[:, 0:1] * ROWS + jnp.sum(twins, axis=-1, keepdims=True)
    at_c = jnp.concatenate([rfl_c + b * SLOTS for b in range(SUB)], axis=0)
    at_r = jnp.broadcast_to(at_c, (SUB * cap, 128)).T[0:1]
    sidx_r = jnp.broadcast_to(sidx_c, (nrow, 128)).T[0:1]
    gvb[...] = jnp.broadcast_to(gates[0].astype(F32), (128, cap)).T

    mine = pl.ds(al(dp * cap, cap), cap)
    gv_all[mine, :] = gvb[...]

    def send_gv(d, carry):
        copy(gvb, gv_all.at[mine], small_s.at[0], small_r.at[0], lax.rem(dp + d, 8)).start()
        return carry

    lax.fori_loop(1, 8, send_gv, 0)
    gv_part = gv_all.at[pl.ds(0, 7 * cap)]
    pending.append(pltpu.make_async_copy(gv_part, gv_part, small_s.at[0]).wait)
    other = pl.ds(al((1 - k) * half, half), half)
    ws0 = push(wg_h.at[0, :, other], wsib.at[0], sib_s.at[0], sib_r.at[0], sib)
    ws1 = push(wu_h.at[0, :, other], wsib.at[1], sib_s.at[1], sib_r.at[1], sib)
    for c in loads:
        c.wait()

    lane_row = lax.broadcasted_iota(jnp.int32, (SUB * cap, nrow), 1).astype(F32)
    ccat[...] = jnp.where(at_c == lane_row, 1.0, 0.0).astype(BF)
    row_i = lax.broadcasted_iota(jnp.int32, (nrow, SUB * cap), 0).astype(F32)
    bcat[...] = jnp.where(at_r == row_i, 1.0, 0.0).astype(BF)
    sub_r = lax.rem(lax.broadcasted_iota(jnp.int32, (tok_rows, nrow), 1) // SLOTS, SUB)
    tok_i = lax.broadcasted_iota(jnp.int32, (tok_rows, nrow), 0).astype(F32)
    tmatch = sidx_r == tok_i
    for b in range(SUB):
        fcat[b * tok_rows : (b + 1) * tok_rows, :] = jnp.where(tmatch & (sub_r == b), 1.0, 0.0).astype(BF)

    hc = cap // 2
    kt = 512
    hops = {}

    def blk(q, i, lo, n):
        return alls.at[q // CH, pl.ds(al(i * cap + lo, 16), n), pl.ds((q % CH) * cw, cw)]

    def pass_on(q, j, i, to, lo=0, n=cap):
        hops[q, j] = push(blk(q, i, lo, n), blk(q, i, lo, n), g_send.at[q, j], g_recv.at[q, j], to)

    def arrive(q):
        await_bytes(recvb.at[q], d_recv.at[q])
        packed = dot(ccat[...], recvb[q]).astype(BF)
        for b in range(SUB):
            col = (q % CH) * cw + b * sw
            alls[q // CH, mine, col : col + sw] = packed[b * cap : (b + 1) * cap]
        pass_on(q, 0, dp, up_d)
        pass_on(q, 1, dp, dn_d)
        pass_on(q, 2, dp, sib)
        if q + DEPTH < 2 * CH:
            dispatch(q + DEPTH)

    def forward(q):
        hops[q, 0].wait_recv()
        pass_on(q, 3, dn_d, up_d, 0, hc)
        pass_on(q, 4, dn_d, sib)
        hops[q, 1].wait_recv()
        pass_on(q, 5, up_d, dn_d, hc, hc)
        pass_on(q, 6, up_d, sib)

    def complete(q):
        hops[q, 3].wait_recv()
        pass_on(q, 7, op_d, sib, 0, hc)
        hops[q, 5].wait_recv()
        pass_on(q, 8, op_d, sib, hc, hc)
        for j in (2, 4, 6, 7, 8):
            hops[q, j].wait_recv()

    def products(q):
        c = q % CH

        def fwd(i, carry):
            kk = pl.ds(al(c * cw + i * kt, kt), kt)
            r = alls[0, :, kk]
            gate[...] += dot_nt(r, wg[:, kk])
            up[...] += dot_nt(r, wu[:, kk])
            return carry

        def bwd(i, carry):
            kk = pl.ds(al(c * cw + i * kt, kt), kt)
            back[...] += dot_nt(alls[1, :, kk], wd[:, kk])
            return carry

        lax.fori_loop(0, cw // kt, fwd if q < CH else bwd, 0)

    def activate(i, carry):
        r = pl.ds(al(i * 128, 128), 128)
        g, u = gate[r, :], up[r, :]
        s = jax.nn.sigmoid(g)
        act = g * s
        hid[r, :] = (act * u).astype(BF)
        gate[r, :] = u * s * (1.0 + g * (1.0 - s))
        up[r, :] = act
        return carry

    for acc in (gate, up, back):
        acc[...] = jnp.zeros_like(acc)
    for q in range(2 * CH):
        arrive(q)
        if q > 0:
            complete(q - 1)
            products(q - 1)
        forward(q)
        if q == CH:
            lax.fori_loop(0, 4, activate, 0)
    complete(2 * CH - 1)
    products(2 * CH - 1)

    pltpu.make_async_copy(gv_part, gv_part, small_r.at[0]).wait()

    def pointwise(i, carry):
        r = pl.ds(al(i * 128, 128), 128)
        dh = gv_all[r, 0:1] * back[r, :]
        dgu[0, r, :] = (dh * gate[r, :]).astype(BF)
        dgu[1, r, :] = (dh * up[r, :]).astype(BF)
        return carry

    lax.fori_loop(0, 4, pointwise, 0)
    dx = push(dgu, dgs, sib_s.at[2], sib_r.at[2], sib)

    two = 2 * cap
    fw = half // RC
    hw = fw // 2

    def part(yy, c, ready=()):
        r = pl.ds(al(yy * two, two), two)
        w_at = pl.ds(al(k * half + c * fw, fw), fw)
        o_at = pl.ds(c * fw, fw)
        t = dot(dgu[0, r, :], wg[:, w_at])
        t += dot(dgu[1, r, :], wu[:, w_at])
        for d in ready:
            d.wait_recv()
        t += dot(dgs[0, r, :], wsib[0, :, o_at])
        t += dot(dgs[1, r, :], wsib[1, :, o_at])
        return t

    a_cp, b_cp, x_cp = {}, {}, {}

    def far_terms(c):
        t = part(y_op, c, (ws0, ws1, dx) if c == 0 else ())
        a_s[c, 0] = t[:, :hw].astype(BF)
        a_s[c, 1] = t[:, hw:].astype(BF)
        for j, to in ((0, up_d), (1, dn_d)):
            a_cp[c, j] = push(a_s.at[c, j], a_r.at[c, j], rs_s.at[c, j], rs_r.at[c, j], to)

    def near_terms(c):
        for j, (yy, to) in enumerate(((y_up, up_d), (y_dn, dn_d))):
            t = part(yy, c)
            a_cp[c, j].wait_recv()
            at = slice(0, hw) if j == 0 else slice(hw, fw)
            rest = slice(hw, fw) if j == 0 else slice(0, hw)
            b_s[c, j, :, at] = (t[:, at] + a_r[c, j].astype(F32)).astype(BF)
            b_s[c, j, :, rest] = t[:, rest].astype(BF)
            b_cp[c, j] = push(b_s.at[c, j], b_r.at[c, j], rs_s.at[c, 2 + j], rs_r.at[c, 2 + j], to)

    def own_sum(c):
        t = part(y, c)
        b_cp[c, 0].wait_recv()
        b_cp[c, 1].wait_recv()
        t += b_r[c, 0].astype(F32) + b_r[c, 1].astype(F32)
        dg_own[c] = t.astype(BF)
        theirs = dg_own.at[c, pl.ds(al((1 - k) * cap, cap), cap)]
        x_cp[c] = push(theirs, dg_x.at[c], rs_s.at[c, 4], rs_r.at[c, 4], sib)

    def give_back(c):
        x_cp[c].wait_recv()
        mine_half = dg_own[c, pl.ds(al(k * cap, cap), cap), :]
        theirs = dg_x[c]
        h0 = jnp.where(k == 0, mine_half, theirs)
        h1 = jnp.where(k == 0, theirs, mine_half)
        stacked = jnp.concatenate([h0[:, :hw], h0[:, hw:], h1[:, :hw], h1[:, hw:]], axis=0)
        ret_s[c] = dot(bcat[...], stacked).astype(BF)
        ret_r[c, own, :] = ret_s[c, own, :]
        spread(ret_s.at[c], ret_r.at[c], r_send.at[c], r_recv.at[c])

    far_terms(0)
    far_terms(1)
    near_terms(0)
    far_terms(2)
    near_terms(1)
    own_sum(0)
    for c in range(RC):
        if c + 3 < RC:
            far_terms(c + 3)
        if c + 2 < RC:
            near_terms(c + 2)
        if c + 1 < RC:
            own_sum(c + 1)
        give_back(c)

    def turn(i, carry):
        r = pl.ds(al(i * 128, 128), 128)
        hidden = hid[r, :].astype(F32)
        total = jnp.sum(hidden * back[r, :], axis=-1, keepdims=True)
        sc_p[r, :] = jnp.broadcast_to(total, (128, 128))
        tr[0, :, r] = hidden.T.astype(BF)
        tr[1, :, r] = dgu[0, r, :].astype(F32).T.astype(BF)
        tr[2, :, r] = dgu[1, r, :].astype(F32).T.astype(BF)
        return carry

    lax.fori_loop(0, 4, turn, 0)

    def send_score(d, carry):
        to = lax.rem(dp + d, 8)
        copy(
            sc_p.at[pl.ds(al(to * cap, cap), cap)], sc_r.at[lax.rem(8 - d, 8)],
            small_s.at[1], small_r.at[1], to,
        ).start()
        return carry

    lax.fori_loop(1, 8, send_score, 0)
    sc_part = sc_r.at[pl.ds(1, 7)]
    pending.append(pltpu.make_async_copy(sc_part, sc_part, small_s.at[1]).wait)

    nt = 512

    def grads(i, carry):
        cc = pl.ds(al(i * nt, nt), nt)
        dyt = alls[1, :, cc].astype(F32)
        d_out = (gv_all[:, 0:1] * dyt).astype(BF)
        dwd[:, cc] = dot(tr[0], d_out).astype(BF)
        r = alls[0, :, cc]
        dwg[:, cc] = dot(tr[1], r).astype(BF)
        dwu[:, cc] = dot(tr[2], r).astype(BF)
        return carry

    lax.fori_loop(0, width // nt, grads, 0)
    stores = [
        pltpu.make_async_copy(v, h.at[0], loc.at[i])
        for i, (h, v) in enumerate(((dwg_h, dwg), (dwu_h, dwu), (dwd_h, dwd)))
    ]
    for c in stores:
        c.start()
    pltpu.make_async_copy(sc_part, sc_part, small_r.at[1]).wait()
    total = sc_p[mine, :]
    for j in range(1, 8):
        total += sc_r[j]
    score[0] = total.T[0:1]

    for c in range(RC):
        await_bytes(ret_r.at[c], r_recv.at[c])
        sums = dot(fcat[...], ret_r[c]).astype(BF)
        for b in range(SUB):
            col = (b // 2) * half + c * fw + (b % 2) * hw
            dtok[:, col : col + hw] = sums[b * tok_rows : (b + 1) * tok_rows]

    for wait in pending:
        wait()
    for c in stores:
        c.wait()


def hand_over(*refs):
    n = (len(refs) - 1) // 2
    copies = [pltpu.make_async_copy(refs[i], refs[n + i], refs[-1].at[i]) for i in range(n)]
    for c in copies:
        c.start()
    for c in copies:
        c.wait()


def on_device(tokens, cotangent, picks, gate_values, w_gate, w_up, w_down):
    tok_rows, width = tokens.shape
    experts = lax.axis_size("expert")
    groups = lax.axis_size("dp")
    ff = w_down.shape[1]
    cap = picks.shape[2]
    nrow = experts * ROWS
    half = width // 2
    cw = width // CH
    fw = half // RC
    rows = groups * cap
    vm = pl.BlockSpec(memory_space=pltpu.VMEM)
    hbm = pl.BlockSpec(memory_space=pl.ANY)
    dma = pltpu.SemaphoreType.DMA
    results = pl.pallas_call(
        functools.partial(kernel, experts),
        out_shape=(
            jax.ShapeDtypeStruct((tok_rows, width), BF),
            jax.ShapeDtypeStruct((1, 1, cap), F32),
            jax.ShapeDtypeStruct((1, ff, width), BF),
            jax.ShapeDtypeStruct((1, ff, width), BF),
            jax.ShapeDtypeStruct(w_down.shape, BF),
        ),
        in_specs=[vm] * 4 + [hbm] * 3,
        out_specs=[vm] * 2 + [hbm] * 3,
        scratch_shapes=[
            pltpu.VMEM((nrow, SUB * tok_rows), BF),
            pltpu.VMEM((SUB * cap, nrow), BF),
            pltpu.VMEM((nrow, SUB * cap), BF),
            pltpu.VMEM((SUB * tok_rows, nrow), BF),
            pltpu.VMEM((2 * CH, nrow, cw // SUB), BF),
            pltpu.VMEM((2 * CH, nrow, cw // SUB), BF),
            pltpu.VMEM((2, rows, width), BF),
            pltpu.VMEM((cap, 128), F32),
            pltpu.VMEM((rows, 128), F32),
            pltpu.VMEM((ff, width), BF),
            pltpu.VMEM((ff, width), BF),
            pltpu.VMEM((ff, width), BF),
            pltpu.VMEM((2, ff, half), BF),
            pltpu.VMEM((rows, ff), F32),
            pltpu.VMEM((rows, ff), F32),
            pltpu.VMEM((rows, ff), F32),
            pltpu.VMEM((rows, ff), BF),
            pltpu.VMEM((2, rows, ff), BF),
            pltpu.VMEM((2, rows, ff), BF),
            pltpu.VMEM((3, ff, rows), BF),
            pltpu.VMEM((RC, 2, 2 * cap, fw // 2), BF),
            pltpu.VMEM((RC, 2, 2 * cap, fw // 2), BF),
            pltpu.VMEM((RC, 2, 2 * cap, fw), BF),
            pltpu.VMEM((RC, 2, 2 * cap, fw), BF),
            pltpu.VMEM((RC, 2 * cap, fw), BF),
            pltpu.VMEM((RC, cap, fw), BF),
            pltpu.VMEM((RC, nrow, fw // 2), BF),
            pltpu.VMEM((RC, nrow, fw // 2), BF),
            pltpu.VMEM((rows, 128), F32),
            pltpu.VMEM((groups, cap, 128), F32),
            pltpu.VMEM((ff, width), BF),
            pltpu.VMEM((ff, width), BF),
            pltpu.VMEM((ff, width), BF),
            dma((2 * CH,)), dma((2 * CH,)),
            dma((2 * CH, 9)), dma((2 * CH, 9)),
            dma((2,)), dma((2,)),
            dma((3,)), dma((3,)),
            dma((RC, 5)), dma((RC, 5)),
            dma((RC,)), dma((RC,)),
            dma((3,)),
        ],
        compiler_params=pltpu.CompilerParams(
            collective_id=0, has_side_effects=True, vmem_limit_bytes=46 * 2**20
        ),
        cost_estimate=pl.CostEstimate(
            flops=2 * 8 * rows * width * ff, bytes_accessed=12 * 2**20, transcendentals=rows * ff
        ),
    )(
        tokens, cotangent, picks, gate_values,
        jnp.swapaxes(w_gate, 1, 2), jnp.swapaxes(w_up, 1, 2), w_down,
    )
    d_tokens, score, dwg, dwu, dwd = pl.pallas_call(
        hand_over,
        out_shape=[jax.ShapeDtypeStruct(r.shape, r.dtype) for r in results],
        in_specs=[vm] * 5,
        out_specs=[hbm] * 5,
        scratch_shapes=[dma((5,))],
        compiler_params=pltpu.CompilerParams(vmem_limit_bytes=16 * 2**20),
    )(*results)
    return d_tokens, score, jnp.swapaxes(dwg, 1, 2), jnp.swapaxes(dwu, 1, 2), dwd


def solution(mesh):
    in_specs = (
        P(("dp", "expert"), None),
        P(("dp", "expert"), None),
        P("dp", None, None),
        P("dp", "expert", None),
        P("expert", None, "dp"),
        P("expert", None, "dp"),
        P("expert", "dp", None),
    )
    out_specs = (
        P(("dp", "expert"), None),
        P("dp", "expert", None),
        P("expert", None, "dp"),
        P("expert", None, "dp"),
        P("expert", "dp", None),
    )
    return jax.shard_map(
        on_device, mesh=mesh, in_specs=in_specs, out_specs=out_specs, check_vma=False
    )
```

```python
import functools

import jax
import jax.numpy as jnp
from jax import lax
from jax.experimental import pallas as pl
from jax.experimental.pallas import tpu as pltpu
from jax.sharding import PartitionSpec as P

MESH = pl.DeviceIdType.MESH
BF = jnp.bfloat16
F32 = jnp.float32
NT = (((1,), (1,)), ((), ()))
SLOTS = 4
SUB = 4
ROWS = SLOTS * SUB
CH = 2
RC = 4
PIECE = 64
DEPTH = 4


def dot(a, b):
    return jnp.dot(a, b, preferred_element_type=F32)


def dot_nt(a, b):
    return lax.dot_general(a, b, NT, preferred_element_type=F32)


def al(i, m):
    return pl.multiple_of(i, m)


def kernel(
    experts, tok, cot, picks, gates, wg_h, wu_h, wd_h,
    dtok, score, dwg_h, dwu_h, dwd_h,
    gcat, ccat, bcat, fcat, sendb, recvb, alls, gvb, gv_all, wg, wu, wd, wsib, gate, up, back, hid, dgu, dgs, tr,
    a_s, a_r, b_s, b_r, dg_own, dg_x, ret_s, ret_r, sc_p, sc_r, dwg, dwu, dwd,
    d_send, d_recv, g_send, g_recv, small_s, small_r, sib_s, sib_r, rs_s, rs_r, r_send, r_recv, loc,
):
    tok_rows, width = tok.shape
    cap = gvb.shape[0]
    dp = lax.axis_index("dp")
    ex = lax.axis_index("expert")
    y = dp // 2
    k = lax.rem(dp, 2)
    y_up, y_dn, y_op = lax.rem(y + 1, 4), lax.rem(y + 3, 4), lax.rem(y + 2, 4)
    up_d, dn_d, op_d, sib = y_up * 2 + k, y_dn * 2 + k, y_op * 2 + k, y * 2 + 1 - k
    half = width // 2
    cw = width // CH
    sw = cw // SUB
    nrow = experts * ROWS

    loads = [
        pltpu.make_async_copy(h.at[0], v, loc.at[i])
        for i, (h, v) in enumerate(((wg_h, wg), (wu_h, wu), (wd_h, wd)))
    ]
    for c in loads:
        c.start()

    pending = []
    barrier = pltpu.get_barrier_semaphore()

    def hail(d, carry):
        pl.semaphore_signal(
            barrier, inc=1, device_id=(dp, lax.rem(ex + d, experts)), device_id_type=MESH
        )
        return carry

    def hail_dp(d, carry):
        pl.semaphore_signal(
            barrier, inc=1, device_id=(lax.rem(dp + d, 8), ex), device_id_type=MESH
        )
        return carry

    lax.fori_loop(1, experts, hail, 0)
    lax.fori_loop(1, 8, hail_dp, 0)

    def copy(src, dst, s, r, to):
        return pltpu.make_async_remote_copy(
            src_ref=src, dst_ref=dst, send_sem=s, recv_sem=r, device_id=(to, ex), device_id_type=MESH
        )

    def push(src, dst, s, r, to):
        d = copy(src, dst, s, r, to)
        d.start()
        pending.append(d.wait_send)
        return d

    def spread(src, dst, s, r):
        def send(d, carry):
            to = lax.rem(ex + d, experts)
            pltpu.make_async_remote_copy(
                src_ref=src.at[pl.ds(al(to * ROWS, ROWS), ROWS)],
                dst_ref=dst.at[pl.ds(al(ex * ROWS, ROWS), ROWS)],
                send_sem=s, recv_sem=r, device_id=(dp, to), device_id_type=MESH,
            ).start()
            return carry

        lax.fori_loop(1, experts, send, 0)
        pending.append(lambda: await_bytes(src, s))

    def await_bytes(ref, sem):
        part = ref.at[pl.ds(0, nrow - ROWS)]
        pltpu.make_async_copy(part, part, sem).wait()

    shift = tok_rows.bit_length() - 1
    lists = picks[0]
    mine_f = jnp.where((lists >> shift) == ex, 1.0, 0.0)
    ahead = lax.broadcasted_iota(jnp.int32, (cap, cap), 0) < lax.broadcasted_iota(jnp.int32, (cap, cap), 1)
    place = dot(mine_f.astype(BF), jnp.where(ahead, 1.0, 0.0).astype(BF))
    token = ((lists & (tok_rows - 1)) + 1).astype(F32) * mine_f
    lane = lax.broadcasted_iota(jnp.int32, (experts, 128), 1)
    slots = jnp.zeros((experts, 128), F32)
    for s in range(SLOTS):
        at = jnp.sum(jnp.where(place == s, token, 0.0), axis=-1, keepdims=True)
        slots = jnp.where(lane == s, at, slots)
    grow = lax.broadcasted_iota(jnp.int32, (nrow, experts), 0) // ROWS
    spot = jnp.where(grow == lax.broadcasted_iota(jnp.int32, (nrow, experts), 1), 1.0, 0.0)
    spread_slots = dot(spot.astype(BF), slots.astype(BF))
    pick_lane = lax.rem(lax.broadcasted_iota(jnp.int32, (nrow, 128), 0), SLOTS)
    at_lane = lax.broadcasted_iota(jnp.int32, (nrow, 128), 1)
    sidx_c = jnp.sum(jnp.where(at_lane == pick_lane, spread_slots, 0.0), axis=-1, keepdims=True) - 1.0

    row_sub = lax.rem(lax.broadcasted_iota(jnp.int32, (nrow, tok_rows), 0) // SLOTS, SUB)
    col_tok = lax.broadcasted_iota(jnp.int32, (nrow, tok_rows), 1)
    match = sidx_c == col_tok.astype(F32)
    for b in range(SUB):
        gcat[:, b * tok_rows : (b + 1) * tok_rows] = jnp.where(match & (row_sub == b), 1.0, 0.0).astype(BF)
    own = pl.ds(al(ex * ROWS, ROWS), ROWS)

    def dispatch(q):
        spread(sendb.at[q], recvb.at[q], d_send.at[q], d_recv.at[q])

    for q in range(2 * CH):
        src = tok if q < CH else cot
        base = (q % CH) * cw
        stacked = jnp.concatenate([src[:, base + b * sw : base + (b + 1) * sw] for b in range(SUB)], axis=0)
        sendb[q] = dot(gcat[...], stacked).astype(BF)
        recvb[q, own, :] = sendb[q, own, :]
        if q == 0:
            pl.semaphore_wait(barrier, experts - 1 + 7)
        if q < DEPTH:
            dispatch(q)

    own_row = picks[0, pl.ds(ex, 1), :]
    src_row = jnp.broadcast_to((own_row >> shift).astype(F32), (128, cap))
    src_col = src_row.T
    behind = lax.broadcasted_iota(jnp.int32, (cap, cap), 0) > lax.broadcasted_iota(jnp.int32, (cap, cap), 1)
    twins = jnp.where((src_col[:, :cap] == src_row[:cap]) & behind, 1.0, 0.0)
    rfl_c = src_col[:, 0:1] * ROWS + jnp.sum(twins, axis=-1, keepdims=True)
    at_c = jnp.concatenate([rfl_c + b * SLOTS for b in range(SUB)], axis=0)
    at_r = jnp.broadcast_to(at_c, (SUB * cap, 128)).T[0:1]
    sidx_r = jnp.broadcast_to(sidx_c, (nrow, 128)).T[0:1]
    gvb[...] = jnp.broadcast_to(gates[0].astype(F32), (128, cap)).T

    mine = pl.ds(al(dp * cap, cap), cap)
    gv_all[mine, :] = gvb[...]

    def send_gv(d, carry):
        copy(gvb, gv_all.at[mine], small_s.at[0], small_r.at[0], lax.rem(dp + d, 8)).start()
        return carry

    lax.fori_loop(1, 8, send_gv, 0)
    gv_part = gv_all.at[pl.ds(0, 7 * cap)]
    pending.append(pltpu.make_async_copy(gv_part, gv_part, small_s.at[0]).wait)
    other = pl.ds(al((1 - k) * half, half), half)
    ws0 = push(wg_h.at[0, :, other], wsib.at[0], sib_s.at[0], sib_r.at[0], sib)
    ws1 = push(wu_h.at[0, :, other], wsib.at[1], sib_s.at[1], sib_r.at[1], sib)
    for c in loads:
        c.wait()

    lane_row = lax.broadcasted_iota(jnp.int32, (SUB * cap, nrow), 1).astype(F32)
    ccat[...] = jnp.where(at_c == lane_row, 1.0, 0.0).astype(BF)
    row_i = lax.broadcasted_iota(jnp.int32, (nrow, SUB * cap), 0).astype(F32)
    bcat[...] = jnp.where(at_r == row_i, 1.0, 0.0).astype(BF)
    sub_r = lax.rem(lax.broadcasted_iota(jnp.int32, (tok_rows, nrow), 1) // SLOTS, SUB)
    tok_i = lax.broadcasted_iota(jnp.int32, (tok_rows, nrow), 0).astype(F32)
    tmatch = sidx_r == tok_i
    for b in range(SUB):
        fcat[b * tok_rows : (b + 1) * tok_rows, :] = jnp.where(tmatch & (sub_r == b), 1.0, 0.0).astype(BF)

    hc = cap // 2
    kt = 512
    hops = {}

    def blk(q, i, lo, n):
        return alls.at[q // CH, pl.ds(al(i * cap + lo, 16), n), pl.ds((q % CH) * cw, cw)]

    def pass_on(q, j, i, to, lo=0, n=cap):
        hops[q, j] = push(blk(q, i, lo, n), blk(q, i, lo, n), g_send.at[q, j], g_recv.at[q, j], to)

    def arrive(q):
        await_bytes(recvb.at[q], d_recv.at[q])
        packed = dot(ccat[...], recvb[q]).astype(BF)
        for b in range(SUB):
            col = (q % CH) * cw + b * sw
            alls[q // CH, mine, col : col + sw] = packed[b * cap : (b + 1) * cap]
        pass_on(q, 0, dp, up_d)
        pass_on(q, 1, dp, dn_d)
        pass_on(q, 2, dp, sib)
        if q + DEPTH < 2 * CH:
            dispatch(q + DEPTH)

    def forward(q):
        hops[q, 0].wait_recv()
        pass_on(q, 3, dn_d, up_d, 0, hc)
        pass_on(q, 4, dn_d, sib)
        hops[q, 1].wait_recv()
        pass_on(q, 5, up_d, dn_d, hc, hc)
        pass_on(q, 6, up_d, sib)

    def complete(q):
        hops[q, 3].wait_recv()
        pass_on(q, 7, op_d, sib, 0, hc)
        hops[q, 5].wait_recv()
        pass_on(q, 8, op_d, sib, hc, hc)
        for j in (2, 4, 6, 7, 8):
            hops[q, j].wait_recv()

    def products(q):
        c = q % CH

        def fwd(i, carry):
            kk = pl.ds(al(c * cw + i * kt, kt), kt)
            r = alls[0, :, kk]
            gate[...] += dot_nt(r, wg[:, kk])
            up[...] += dot_nt(r, wu[:, kk])
            return carry

        def bwd(i, carry):
            kk = pl.ds(al(c * cw + i * kt, kt), kt)
            back[...] += dot_nt(alls[1, :, kk], wd[:, kk])
            return carry

        lax.fori_loop(0, cw // kt, fwd if q < CH else bwd, 0)

    def activate(i, carry):
        r = pl.ds(al(i * 128, 128), 128)
        g, u = gate[r, :], up[r, :]
        s = jax.nn.sigmoid(g)
        act = g * s
        hid[r, :] = (act * u).astype(BF)
        gate[r, :] = u * s * (1.0 + g * (1.0 - s))
        up[r, :] = act
        return carry

    for acc in (gate, up, back):
        acc[...] = jnp.zeros_like(acc)
    for q in range(2 * CH):
        arrive(q)
        if q > 0:
            complete(q - 1)
            products(q - 1)
        forward(q)
        if q == CH:
            lax.fori_loop(0, 4, activate, 0)
    complete(2 * CH - 1)
    products(2 * CH - 1)

    pltpu.make_async_copy(gv_part, gv_part, small_r.at[0]).wait()

    def pointwise(i, carry):
        r = pl.ds(al(i * 128, 128), 128)
        dh = gv_all[r, 0:1] * back[r, :]
        dgu[0, r, :] = (dh * gate[r, :]).astype(BF)
        dgu[1, r, :] = (dh * up[r, :]).astype(BF)
        return carry

    lax.fori_loop(0, 4, pointwise, 0)
    dx = push(dgu, dgs, sib_s.at[2], sib_r.at[2], sib)

    two = 2 * cap
    fw = half // RC
    hw = fw // 2

    def part(yy, c, ready=()):
        r = pl.ds(al(yy * two, two), two)
        w_at = pl.ds(al(k * half + c * fw, fw), fw)
        o_at = pl.ds(c * fw, fw)
        t = dot(dgu[0, r, :], wg[:, w_at])
        t += dot(dgu[1, r, :], wu[:, w_at])
        for d in ready:
            d.wait_recv()
        t += dot(dgs[0, r, :], wsib[0, :, o_at])
        t += dot(dgs[1, r, :], wsib[1, :, o_at])
        return t

    a_cp, b_cp, x_cp = {}, {}, {}

    def far_terms(c):
        t = part(y_op, c, (ws0, ws1, dx) if c == 0 else ())
        a_s[c, 0] = t[:, :hw].astype(BF)
        a_s[c, 1] = t[:, hw:].astype(BF)
        for j, to in ((0, up_d), (1, dn_d)):
            a_cp[c, j] = push(a_s.at[c, j], a_r.at[c, j], rs_s.at[c, j], rs_r.at[c, j], to)

    def near_terms(c):
        for j, (yy, to) in enumerate(((y_up, up_d), (y_dn, dn_d))):
            t = part(yy, c)
            a_cp[c, j].wait_recv()
            at = slice(0, hw) if j == 0 else slice(hw, fw)
            rest = slice(hw, fw) if j == 0 else slice(0, hw)
            b_s[c, j, :, at] = (t[:, at] + a_r[c, j].astype(F32)).astype(BF)
            b_s[c, j, :, rest] = t[:, rest].astype(BF)
            b_cp[c, j] = push(b_s.at[c, j], b_r.at[c, j], rs_s.at[c, 2 + j], rs_r.at[c, 2 + j], to)

    def own_sum(c):
        t = part(y, c)
        b_cp[c, 0].wait_recv()
        b_cp[c, 1].wait_recv()
        t += b_r[c, 0].astype(F32) + b_r[c, 1].astype(F32)
        dg_own[c] = t.astype(BF)
        theirs = dg_own.at[c, pl.ds(al((1 - k) * cap, cap), cap)]
        x_cp[c] = push(theirs, dg_x.at[c], rs_s.at[c, 4], rs_r.at[c, 4], sib)

    def give_back(c):
        x_cp[c].wait_recv()
        mine_half = dg_own[c, pl.ds(al(k * cap, cap), cap), :]
        theirs = dg_x[c]
        h0 = jnp.where(k == 0, mine_half, theirs)
        h1 = jnp.where(k == 0, theirs, mine_half)
        stacked = jnp.concatenate([h0[:, :hw], h0[:, hw:], h1[:, :hw], h1[:, hw:]], axis=0)
        ret_s[c] = dot(bcat[...], stacked).astype(BF)
        ret_r[c, own, :] = ret_s[c, own, :]
        spread(ret_s.at[c], ret_r.at[c], r_send.at[c], r_recv.at[c])

    far_terms(0)
    far_terms(1)
    near_terms(0)
    far_terms(2)
    near_terms(1)
    own_sum(0)
    for c in range(RC):
        if c + 3 < RC:
            far_terms(c + 3)
        if c + 2 < RC:
            near_terms(c + 2)
        if c + 1 < RC:
            own_sum(c + 1)
        give_back(c)

    def turn(i, carry):
        r = pl.ds(al(i * 128, 128), 128)
        hidden = hid[r, :].astype(F32)
        total = jnp.sum(hidden * back[r, :], axis=-1, keepdims=True)
        sc_p[r, :] = jnp.broadcast_to(total, (128, 128))
        tr[0, :, r] = hidden.T.astype(BF)
        tr[1, :, r] = dgu[0, r, :].astype(F32).T.astype(BF)
        tr[2, :, r] = dgu[1, r, :].astype(F32).T.astype(BF)
        return carry

    lax.fori_loop(0, 4, turn, 0)

    def send_score(d, carry):
        to = lax.rem(dp + d, 8)
        copy(
            sc_p.at[pl.ds(al(to * cap, cap), cap)], sc_r.at[lax.rem(8 - d, 8)],
            small_s.at[1], small_r.at[1], to,
        ).start()
        return carry

    lax.fori_loop(1, 8, send_score, 0)
    sc_part = sc_r.at[pl.ds(1, 7)]
    pending.append(pltpu.make_async_copy(sc_part, sc_part, small_s.at[1]).wait)

    nt = 512

    def grads(i, carry):
        cc = pl.ds(al(i * nt, nt), nt)
        dyt = alls[1, :, cc].astype(F32)
        d_out = (gv_all[:, 0:1] * dyt).astype(BF)
        dwd[:, cc] = dot(tr[0], d_out).astype(BF)
        r = alls[0, :, cc]
        dwg[:, cc] = dot(tr[1], r).astype(BF)
        dwu[:, cc] = dot(tr[2], r).astype(BF)
        return carry

    lax.fori_loop(0, width // nt, grads, 0)
    stores = [
        pltpu.make_async_copy(v, h.at[0], loc.at[i])
        for i, (h, v) in enumerate(((dwg_h, dwg), (dwu_h, dwu), (dwd_h, dwd)))
    ]
    for c in stores:
        c.start()
    pltpu.make_async_copy(sc_part, sc_part, small_r.at[1]).wait()
    total = sc_p[mine, :]
    for j in range(1, 8):
        total += sc_r[j]
    score[0] = total.T[0:1]

    for c in range(RC):
        await_bytes(ret_r.at[c], r_recv.at[c])
        sums = dot(fcat[...], ret_r[c]).astype(BF)
        for b in range(SUB):
            col = (b // 2) * half + c * fw + (b % 2) * hw
            dtok[:, col : col + hw] = sums[b * tok_rows : (b + 1) * tok_rows]

    for wait in pending:
        wait()
    for c in stores:
        c.wait()


def hand_over(*refs):
    n = (len(refs) - 1) // 2
    copies = [pltpu.make_async_copy(refs[i], refs[n + i], refs[-1].at[i]) for i in range(n)]
    for c in copies:
        c.start()
    for c in copies:
        c.wait()


def on_device(tokens, cotangent, picks, gate_values, w_gate, w_up, w_down):
    tok_rows, width = tokens.shape
    experts = lax.axis_size("expert")
    groups = lax.axis_size("dp")
    ff = w_down.shape[1]
    cap = picks.shape[2]
    nrow = experts * ROWS
    half = width // 2
    cw = width // CH
    fw = half // RC
    rows = groups * cap
    vm = pl.BlockSpec(memory_space=pltpu.VMEM)
    hbm = pl.BlockSpec(memory_space=pl.ANY)
    dma = pltpu.SemaphoreType.DMA
    results = pl.pallas_call(
        functools.partial(kernel, experts),
        out_shape=(
            jax.ShapeDtypeStruct((tok_rows, width), BF),
            jax.ShapeDtypeStruct((1, 1, cap), F32),
            jax.ShapeDtypeStruct((1, ff, width), BF),
            jax.ShapeDtypeStruct((1, ff, width), BF),
            jax.ShapeDtypeStruct(w_down.shape, BF),
        ),
        in_specs=[vm] * 4 + [hbm] * 3,
        out_specs=[vm] * 2 + [hbm] * 3,
        scratch_shapes=[
            pltpu.VMEM((nrow, SUB * tok_rows), BF),
            pltpu.VMEM((SUB * cap, nrow), BF),
            pltpu.VMEM((nrow, SUB * cap), BF),
            pltpu.VMEM((SUB * tok_rows, nrow), BF),
            pltpu.VMEM((2 * CH, nrow, cw // SUB), BF),
            pltpu.VMEM((2 * CH, nrow, cw // SUB), BF),
            pltpu.VMEM((2, rows, width), BF),
            pltpu.VMEM((cap, 128), F32),
            pltpu.VMEM((rows, 128), F32),
            pltpu.VMEM((ff, width), BF),
            pltpu.VMEM((ff, width), BF),
            pltpu.VMEM((ff, width), BF),
            pltpu.VMEM((2, ff, half), BF),
            pltpu.VMEM((rows, ff), F32),
            pltpu.VMEM((rows, ff), F32),
            pltpu.VMEM((rows, ff), F32),
            pltpu.VMEM((rows, ff), BF),
            pltpu.VMEM((2, rows, ff), BF),
            pltpu.VMEM((2, rows, ff), BF),
            pltpu.VMEM((3, ff, rows), BF),
            pltpu.VMEM((RC, 2, 2 * cap, fw // 2), BF),
            pltpu.VMEM((RC, 2, 2 * cap, fw // 2), BF),
            pltpu.VMEM((RC, 2, 2 * cap, fw), BF),
            pltpu.VMEM((RC, 2, 2 * cap, fw), BF),
            pltpu.VMEM((RC, 2 * cap, fw), BF),
            pltpu.VMEM((RC, cap, fw), BF),
            pltpu.VMEM((RC, nrow, fw // 2), BF),
            pltpu.VMEM((RC, nrow, fw // 2), BF),
            pltpu.VMEM((rows, 128), F32),
            pltpu.VMEM((groups, cap, 128), F32),
            pltpu.VMEM((ff, width), BF),
            pltpu.VMEM((ff, width), BF),
            pltpu.VMEM((ff, width), BF),
            dma((2 * CH,)), dma((2 * CH,)),
            dma((2 * CH, 9)), dma((2 * CH, 9)),
            dma((2,)), dma((2,)),
            dma((3,)), dma((3,)),
            dma((RC, 5)), dma((RC, 5)),
            dma((RC,)), dma((RC,)),
            dma((3,)),
        ],
        compiler_params=pltpu.CompilerParams(
            collective_id=0, has_side_effects=True, vmem_limit_bytes=46 * 2**20
        ),
        cost_estimate=pl.CostEstimate(
            flops=2 * 8 * rows * width * ff, bytes_accessed=12 * 2**20, transcendentals=rows * ff
        ),
    )(
        tokens, cotangent, picks, gate_values,
        jnp.swapaxes(w_gate, 1, 2), jnp.swapaxes(w_up, 1, 2), w_down,
    )
    d_tokens, score, dwg, dwu, dwd = pl.pallas_call(
        hand_over,
        out_shape=[jax.ShapeDtypeStruct(r.shape, r.dtype) for r in results],
        in_specs=[vm] * 5,
        out_specs=[hbm] * 5,
        scratch_shapes=[dma((5,))],
        compiler_params=pltpu.CompilerParams(vmem_limit_bytes=16 * 2**20),
    )(*results)
    return d_tokens, score, jnp.swapaxes(dwg, 1, 2), jnp.swapaxes(dwu, 1, 2), dwd


def solution(mesh):
    in_specs = (
        P(("dp", "expert"), None),
        P(("dp", "expert"), None),
        P("dp", None, None),
        P("dp", "expert", None),
        P("expert", None, "dp"),
        P("expert", None, "dp"),
        P("expert", "dp", None),
    )
    out_specs = (
        P(("dp", "expert"), None),
        P("dp", "expert", None),
        P("expert", None, "dp"),
        P("expert", None, "dp"),
        P("expert", "dp", None),
    )
    return jax.shard_map(
        on_device, mesh=mesh, in_specs=in_specs, out_specs=out_specs, check_vma=False
    )
```
